128 devices in a mesh: layer: 2 (over core), feat: 64 (over y, x, z).
Axes of the slice: x: 4, y: 4, z: 4, core: 2. Of those that a mesh axis runs over, the one named last changes fastest.
Arguments:
- inputs: bfloat16 [2, 512, 4608], P('layer', 'feat'), may hold values from -6 to 6
- targets: bfloat16 [2, 512, 4608], P('layer', 'feat'), may hold values from -6 to 6
- w_enc: bfloat16 [2, 4608, 32768], P('layer', None, 'feat'), may hold values from -0.09375 to 0.09375
- b_enc: float32 [2, 32768], P('layer', 'feat'), may hold values from -4 to 4
- w_self: bfloat16 [2, 32768, 4608], P('layer', 'feat'), may hold values from -0.1875 to 0.1875
- w_cross: bfloat16 [32768, 4608], P('feat', 'layer'), may hold values from -0.1875 to 0.1875
- block_ids: int32 [2, 512, 8], P('layer', 'feat'), may hold values from 0 to 255, all different within a row
Outputs:
- reconstruction: float32 [2, 512, 4608], P('layer', 'feat')
- active_codes: bfloat16 [2, 512, 8, 128], P('layer', 'feat')
- grad_enc: bfloat16 [2, 4608, 32768], P('layer', None, 'feat')
- grad_benc: float32 [2, 32768], P('layer', 'feat')
- grad_self: bfloat16 [2, 32768, 4608], P('layer', 'feat')
- grad_cross: bfloat16 [32768, 4608], P('feat', 'layer')
The draws below stay inside these ranges and needn't reach their ends.
Inputs may be any that keep to these rules, and one draw needn't show every extreme that they name: `block_ids`: each token names 8 different blocks in each layer; every block is named by some token of the two layers taken together.
All inputs are finite; a program needn't handle non-finite values.
Results may differ from the reference program's by a relative error of at most 0.0058.
Values may be sent and summed in bfloat16 or wider, within the bound.
No kernel may reach another device: no remote copies, remote signals or barrier semaphores. Data moves between devices by JAX's collectives and lax.ppermute only.
A program may use at most 128 MiB of HBM per device.

```python
import jax
import jax.numpy as jnp
from jax import lax

D = 4608
F = 32768
BLK = 128
K = 8
TOKENS = 512


def level_of(rng, dims, cuts, smallest, largest):
    def one(dim, parts):
        steps = jax.random.uniform(jax.random.fold_in(jax.random.fold_in(rng, 6), dim), (parts,), jnp.float32, smallest / len(cuts), largest / len(cuts))
        return jnp.repeat(jnp.exp(steps), dims[dim] // parts).reshape((-1,) + (1,) * (len(dims) - dim - 1))

    gain = one(*cuts[0])
    for cut in cuts[1:]:
        gain = gain * one(*cut)
    return gain


def distinct(key, rows, amount, top, lift):
    order = jax.random.permutation(jax.random.fold_in(key, 1), amount)
    favour = order
    for power in range(3):
        favour = favour * favour // amount
    favour = favour * lift // amount
    chance = jax.random.randint(jax.random.fold_in(key, 2), (rows, amount), 0, 4096) + favour
    fixed_rows = jax.random.permutation(jax.random.fold_in(key, 3), rows)[jnp.arange(amount) % rows]
    chance = jnp.where(jnp.arange(rows)[:, None] == fixed_rows[None, :], 1 << 14, chance)
    priority = chance * amount + jnp.arange(amount)
    return lax.top_k(priority.astype(jnp.int32), top)[1].astype(jnp.int32)


def gaussian(rng, shape, scale, limit, split=(), held_as=jnp.bfloat16):
    array = scale * jax.random.normal(rng, shape, jnp.float32)
    if split:
        array = array * level_of(rng, shape, split, -0.22, 0.18)
    return jnp.clip(array, -limit, limit).astype(held_as)


def setup_inputs(seed: int = 0) -> dict:
    key_of = jax.random.split(jax.random.key(seed), 8)
    inputs = gaussian(key_of[0], (2, TOKENS, D), 1.0, 6.0, ((0, 2), (1, 64)))
    targets = gaussian(key_of[1], (2, TOKENS, D), 1.0, 6.0, ((0, 2), (1, 64)))
    w_enc = gaussian(key_of[2], (2, D, F), D ** -0.5, 0.09375, ((0, 2), (2, 64)))
    b_enc = gaussian(key_of[3], (2, F), 1.0, 4.0, ((0, 2), (1, 64)), jnp.float32)
    w_self = gaussian(key_of[4], (2, F, D), (K * BLK) ** -0.5, 0.1875, ((0, 2), (1, 64)))
    w_cross = gaussian(key_of[5], (F, D), (K * BLK) ** -0.5, 0.1875, ((0, 64), (1, 2)))
    block_ids = distinct(key_of[6], 2 * TOKENS, F // BLK, K, 256).reshape((2, TOKENS, K))
    return dict(inputs=inputs, targets=targets, w_enc=w_enc, b_enc=b_enc, w_self=w_self, w_cross=w_cross, block_ids=block_ids)


def reference(inputs, targets, w_enc, b_enc, w_self, w_cross, block_ids):
    block_count = F // BLK
    numbers = jnp.arange(block_count, dtype=jnp.int32)
    actives = []
    pre_list = []
    code_list = []
    for source_layer in range(2):
        table = jnp.any(block_ids[source_layer][:, :, None] == numbers[None, None, :], axis=1)
        active = jnp.repeat(table.astype(jnp.float32), BLK, axis=1)
        pre_acts = jnp.dot(inputs[source_layer], w_enc[source_layer], preferred_element_type=jnp.float32) + b_enc[source_layer]
        latent_codes = (active * jax.nn.softplus(pre_acts)).astype(jnp.bfloat16)
        actives.append(active)
        pre_list.append(pre_acts)
        code_list.append(latent_codes)
    recon_first = jnp.dot(code_list[0], w_self[0], preferred_element_type=jnp.float32)
    recon_second = jnp.dot(code_list[1], w_self[1], preferred_element_type=jnp.float32) + jnp.dot(code_list[0], w_cross, preferred_element_type=jnp.float32)
    recons = [recon_first, recon_second]
    errors = [(recons[i] - targets[i].astype(jnp.float32)).astype(jnp.bfloat16) for i in range(2)]
    grad_self = jnp.stack([jnp.dot(code_list[i].T, errors[i], preferred_element_type=jnp.float32).astype(jnp.bfloat16) for i in range(2)])
    grad_cross = jnp.dot(code_list[0].T, errors[1], preferred_element_type=jnp.float32).astype(jnp.bfloat16)
    grads_first = jnp.dot(errors[0], w_self[0].T, preferred_element_type=jnp.float32) + jnp.dot(errors[1], w_cross.T, preferred_element_type=jnp.float32)
    grads_second = jnp.dot(errors[1], w_self[1].T, preferred_element_type=jnp.float32)
    code_grads = [grads_first, grads_second]
    enc_list = []
    bias_list = []
    picked_list = []
    row_index = jnp.arange(TOKENS, dtype=jnp.int32)[:, None]
    for source_layer in range(2):
        pre_grads = (code_grads[source_layer] * actives[source_layer] * jax.nn.sigmoid(pre_list[source_layer])).astype(jnp.bfloat16)
        enc_list.append(jnp.dot(inputs[source_layer].T, pre_grads, preferred_element_type=jnp.float32).astype(jnp.bfloat16))
        bias_list.append(jnp.sum(pre_grads.astype(jnp.float32), axis=0))
        blocks = code_list[source_layer].reshape(TOKENS, block_count, BLK)
        picked_list.append(blocks[row_index, block_ids[source_layer]])
    reconstruction = jnp.stack(recons)
    active_codes = jnp.stack(picked_list)
    grad_enc = jnp.stack(enc_list)
    grad_benc = jnp.stack(bias_list)
    return reconstruction, active_codes, grad_enc, grad_benc, grad_self, grad_cross
```

```python
import jax
import jax.numpy as jnp
from jax import lax
from jax.sharding import PartitionSpec as P

BLK = 128
SIDE = 4
STEPS = {"y": (1, 0, 0), "x": (0, 1, 0), "z": (0, 0, 1)}


def route(axes, distance):
    pairs = []
    for core, axis in enumerate(axes):
        step = STEPS[axis]
        for y in range(SIDE):
            for x in range(SIDE):
                for z in range(SIDE):
                    there = [(c + distance * s) % SIDE for c, s in zip((y, x, z), step)]
                    base = core * SIDE**3
                    pairs.append(
                        (base + (y * SIDE + x) * SIDE + z, base + (there[0] * SIDE + there[1]) * SIDE + there[2])
                    )
    return pairs


def send(block, axes, distance):
    return lax.ppermute(block, ("layer", "feat"), route(axes, distance))


OUTER = ("z", "y")
MIDDLE = ("x", "x")
INNER = ("y", "z")


def line_gather(block, axes):
    return jnp.stack([block] + [send(block, axes, -r) for r in (1, 2, 3)])


def line_reduce(terms, axes):
    total = terms[0].astype(jnp.float32)
    for r in (1, 2, 3):
        total = total + send(terms[r].astype(jnp.bfloat16), axes, r).astype(jnp.float32)
    return total


def gather_tokens(rows, cut):
    inner = line_gather(rows, INNER)
    first, second = inner[..., :cut], inner[..., cut:]
    second = line_gather(second, OUTER)
    first = line_gather(first, MIDDLE)
    second = line_gather(second, MIDDLE)
    first = line_gather(first, OUTER)
    second = jnp.swapaxes(second, 0, 1)
    return first.reshape(-1, first.shape[-1]), second.reshape(-1, second.shape[-1])


def reduce_tokens(first, second):
    first = first.reshape(SIDE, SIDE, SIDE, -1, first.shape[-1])
    second = second.reshape(SIDE, SIDE, SIDE, -1, second.shape[-1])
    second = line_reduce([second[:, r] for r in range(SIDE)], MIDDLE)
    first = line_reduce([first[r] for r in range(SIDE)], OUTER)
    second = line_reduce([second[r] for r in range(SIDE)], OUTER)
    first = line_reduce([first[r] for r in range(SIDE)], MIDDLE)
    both = jnp.concatenate([first, second], axis=-1)
    return line_reduce([both[r] for r in range(SIDE)], INNER)


def other_order(rows):
    shape = (SIDE, SIDE, SIDE, -1, rows.shape[-1])
    return jnp.transpose(rows.reshape(shape), (2, 1, 0, 3, 4)).reshape(rows.shape)


def to_second(block):
    return lax.ppermute(block, "layer", [(0, 1)])


def to_first(block):
    return lax.ppermute(block, "layer", [(1, 0)])


def contract_rows(left, right):
    return lax.dot_general(left, right, (((0,), (0,)), ((), ())), preferred_element_type=jnp.float32)


def contract_cols(left, right):
    return lax.dot_general(left, right, (((1,), (1,)), ((), ())), preferred_element_type=jnp.float32)


def per_device(inputs, targets, w_enc, b_enc, w_self, w_cross, block_ids):
    first_layer = lax.axis_index("layer") == 0
    shard_index = lax.axis_index("feat")
    width = inputs.shape[2]
    half = width // 2
    latent_dev = w_enc.shape[2]
    blocks_dev = latent_dev // BLK
    slots = block_ids.shape[2]
    tokens_dev = inputs.shape[1]

    w_cross_first = to_second(w_cross)

    ids_bf = jnp.pad(block_ids[0].astype(jnp.bfloat16), ((0, 0), (0, BLK - slots)))
    cut = (2 * width // 3) // BLK * BLK
    x_first, x_second = gather_tokens(jnp.concatenate([inputs[0], ids_bf], axis=1), cut)
    ids = x_second[:, width - cut : width - cut + slots].astype(jnp.int32)
    x_second = x_second[:, : width - cut]
    tokens = x_first.shape[0]

    own_blocks = shard_index * blocks_dev + jnp.arange(blocks_dev, dtype=jnp.int32)
    hit = ids[:, :, None] == own_blocks[None, None, :]
    active = jnp.repeat(jnp.any(hit, axis=1), BLK, axis=1).astype(jnp.float32)
    x_all = jnp.concatenate([x_first, x_second], axis=1)
    pre = jnp.dot(x_all, w_enc[0], preferred_element_type=jnp.float32) + b_enc[0]
    codes = (active * jax.nn.softplus(pre)).astype(jnp.bfloat16)

    codes_turned = other_order(codes)
    earlier = to_second(codes_turned)
    source = jnp.where(first_layer, codes_turned, earlier)

    by_block = codes.reshape(tokens, 1, blocks_dev, BLK)
    slotted = jnp.sum(jnp.where(hit[..., None], by_block, 0).astype(jnp.float32), axis=2)
    slotted = slotted.reshape(tokens, slots * BLK)

    w_cross_all = jnp.concatenate([w_cross_first, w_cross], axis=1)
    self_part = jnp.dot(codes, w_self[0], preferred_element_type=jnp.float32)
    cross_part = jnp.dot(earlier, w_cross_all, preferred_element_type=jnp.float32)
    partial = self_part + jnp.where(first_layer, 0.0, cross_part)

    total_cols = width + slots * BLK
    rcut = (2 * total_cols // 3) // BLK * BLK
    summed = reduce_tokens(
        partial[:, :rcut], jnp.concatenate([partial[:, rcut:], slotted], axis=1)
    )
    recon_rows = summed[:, :width]
    picked = summed[:, width:].astype(jnp.bfloat16).reshape(tokens_dev, slots, BLK)

    err_own = (recon_rows - targets[0].astype(jnp.float32)).astype(jnp.bfloat16)
    err_first, err_second = gather_tokens(err_own, cut)
    err = jnp.concatenate([err_first, err_second], axis=1)

    cross_term = contract_cols(err, w_cross_all)
    back_term = other_order(to_first(cross_term))
    returned = to_first(err[:, :half])
    self_term = contract_cols(err, w_self[0])
    grad_self = contract_rows(codes, err).astype(jnp.bfloat16)
    cross_err = jnp.where(first_layer, returned, err[:, half:])
    grad_cross = contract_rows(source, cross_err).astype(jnp.bfloat16)
    code_grads = self_term + jnp.where(first_layer, back_term, 0.0)
    pre_grads = (code_grads * active * jax.nn.sigmoid(pre)).astype(jnp.bfloat16)
    grad_enc = contract_rows(x_all, pre_grads).astype(jnp.bfloat16)
    grad_benc = jnp.sum(pre_grads.astype(jnp.float32), axis=0)
    return (
        recon_rows[None],
        picked[None],
        grad_enc[None],
        grad_benc[None],
        grad_self[None],
        grad_cross,
    )


def solution(mesh):
    placed = (
        P("layer", "feat", None),
        P("layer", "feat", None),
        P("layer", None, "feat"),
        P("layer", "feat"),
        P("layer", "feat", None),
        P("feat", "layer"),
        P("layer", "feat", None),
    )
    return jax.shard_map(
        per_device,
        mesh=mesh,
        in_specs=placed,
        out_specs=(
            P("layer", "feat", None),
            P("layer", "feat", None, None),
            P("layer", None, "feat"),
            P("layer", "feat"),
            P("layer", "feat", None),
            P("feat", "layer"),
        ),
        check_vma=False,
    )
```

```python
import functools

import jax
import jax.numpy as jnp
from jax import lax
from jax.experimental import pallas as pl
from jax.experimental.pallas import tpu as pltpu
from jax.sharding import PartitionSpec as P

BLK = 128
SIDE = 4
LINE = 32
PLANE = 128
CAP = 64
ROWS = SIDE * CAP
AWAY = (0, 2, 1, 3)
STEPS = {"y": (1, 0, 0), "x": (0, 1, 0), "z": (0, 0, 1)}
F32, BF16 = jnp.float32, jnp.bfloat16

OUTER = ("z", "y")
MIDDLE = ("x", "z")
INNER = ("y", "x")

PARAMS = pltpu.CompilerParams(vmem_limit_bytes=20 * 2**20)


def route(axes, distance):
    pairs = []
    for core, axis in enumerate(axes):
        step = STEPS[axis]
        for y in range(SIDE):
            for x in range(SIDE):
                for z in range(SIDE):
                    there = [(c + distance * s) % SIDE for c, s in zip((y, x, z), step)]
                    base = core * SIDE**3
                    pairs.append(
                        (base + (y * SIDE + x) * SIDE + z, base + (there[0] * SIDE + there[1]) * SIDE + there[2])
                    )
    return pairs


def send(block, axes, distance):
    return lax.ppermute(block, ("layer", "feat"), route(axes, distance))


def ahead(block, pieces, axes):
    return [block] + [send(pieces[r], axes, -AWAY[r]) for r in (1, 2, 3)]


def behind(pieces, axes):
    return [pieces[0]] + [send(pieces[r], axes, AWAY[r]) for r in (1, 2, 3)]


def to_second(block):
    return lax.ppermute(block, "layer", [(0, 1)])


def to_first(block):
    return lax.ppermute(block, "layer", [(1, 0)])


def swapped(block):
    return lax.ppermute(block, "layer", [(0, 1), (1, 0)])


def line_gather(block, axes):
    return ahead(block, [block] * SIDE, axes)


def line_reduce(terms, axes):
    terms = behind([terms[0]] + [term.astype(BF16) for term in terms[1:]], axes)
    return sum(term.astype(F32) for term in terms)


def contract_rows(left, right):
    return lax.dot_general(left, right, (((0,), (0,)), ((), ())), preferred_element_type=F32)


def contract_cols(left, right):
    return lax.dot_general(left, right, (((1,), (1,)), ((), ())), preferred_element_type=F32)


def dot(left, right):
    return jnp.dot(left, right, preferred_element_type=F32)


def call(kernel, name, scalars, ins, outs, scratch=()):
    size = sum(a.size * a.dtype.itemsize for a in ins)
    vmem, smem = pl.BlockSpec(memory_space=pltpu.VMEM), pl.BlockSpec(memory_space=pltpu.SMEM)
    return pl.pallas_call(
        kernel,
        in_specs=[smem] + [vmem] * len(ins),
        out_specs=[pl.BlockSpec(memory_space=out[2]) if len(out) > 2 else vmem for out in outs],
        out_shape=[jax.ShapeDtypeStruct(out[0], out[1]) for out in outs],
        scratch_shapes=list(scratch),
        compiler_params=PARAMS,
        cost_estimate=pl.CostEstimate(flops=2**31, bytes_accessed=size, transcendentals=0),
        name=name,
    )(scalars, *ins)


class Writer:
    def __init__(self, sems):
        self.sems, self.started = sems, []

    def write(self, source, target):
        copy = pltpu.make_async_copy(source, target, self.sems.at[len(self.started)])
        copy.start()
        self.started.append(copy)

    def finish(self):
        for copy in self.started:
            copy.wait()


def sixths(width):
    step = width // 6
    return [pl.ds(j * step, step) for j in range(6)]


def stacked(pieces, cols):
    return jnp.concatenate([p[:, cols] for p in pieces], axis=0)


OWNER_AT, PLACE_AT, FLAG_AT = 16, 17, 18


def select_kernel(s, *refs):
    pieces, outs = refs[:4], refs[4:8]
    pick_ref, spread_ref, flag_ref = refs[8:11]
    width = pieces[0].shape[1]
    tail = jnp.concatenate([p[:, width - BLK :] for p in pieces], axis=0).astype(F32)
    lane = lax.broadcasted_iota(jnp.int32, (PLANE, BLK), 1)
    row = lax.broadcasted_iota(jnp.int32, (PLANE, BLK), 0)
    numbers = jnp.where(lane < OWNER_AT, tail, 0.0)
    needs = jnp.zeros((PLANE, BLK), F32)
    for r in range(SIDE):
        low = (s[2 + r] * 4).astype(F32)
        inside = jnp.where((numbers > low + 0.5) & (numbers < low + 4.5), 1.0, 0.0)
        needs = jnp.where(lane == r, jnp.max(inside, axis=1, keepdims=True), needs)
    needs = needs.astype(BF16)
    upto = jnp.where(row <= lane, 1.0, 0.0).astype(BF16)
    same = jnp.where(row == lane, 1.0, 0.0).astype(BF16)
    down = jnp.where(lane <= row, 1.0, 0.0).astype(BF16)
    count_rows = contract_rows(needs, upto)
    need_rows = contract_rows(needs, same)
    count_cols = dot(down, needs)
    need_cols = needs.astype(F32)
    place = lax.broadcasted_iota(jnp.int32, (CAP, BLK), 0).astype(F32) + 1.0
    for r in range(SIDE):
        hit = (count_rows[r : r + 1, :] == place) & (need_rows[r : r + 1, :] > 0.5)
        pick_ref[pl.ds(r * CAP, CAP), :] = jnp.where(hit, 1.0, 0.0).astype(BF16)
    half = lane < CAP
    place = jnp.where(half, lane, lane - CAP).astype(F32) + 1.0
    for pair in range(2):
        a, b = 2 * pair, 2 * pair + 1
        count = jnp.where(half, count_cols[:, a : a + 1], count_cols[:, b : b + 1])
        need = jnp.where(half, need_cols[:, a : a + 1], need_cols[:, b : b + 1])
        hit = (count == place) & (need > 0.5)
        spread_ref[:, pl.ds(pair * BLK, BLK)] = jnp.where(hit, 1.0, 0.0).astype(BF16)
    most = jnp.max(jnp.max(count_cols, axis=1, keepdims=True), axis=0, keepdims=True)
    flag_ref[...] = jnp.broadcast_to(jnp.where(most > CAP + 0.5, 1.0, 0.0), flag_ref.shape).astype(BF16)
    pick = pick_ref[...]
    for at in range(0, width, 1024):
        cols = pl.ds(at, min(1024, width - at))
        plane = jnp.concatenate([p[:, cols] for p in pieces], axis=0)
        chosen = dot(pick, plane).astype(BF16)
        for r in range(SIDE):
            outs[r][:, cols] = chosen[r * CAP : (r + 1) * CAP]


def select(scalars, pieces):
    width = pieces[0].shape[1]
    outs = [((CAP, width), BF16)] * 4 + [((ROWS, PLANE), BF16), ((PLANE, ROWS), BF16), ((CAP, BLK), BF16)]
    *chosen, pick, spread, flag = call(select_kernel, "select", scalars, pieces, outs)
    return chosen, pick, spread, flag


def encode_kernel(slots, s, *refs):
    pieces, w_ref, b_ref, flag_ref = refs[:4], *refs[4:7]
    codes_ref, gate_ref, acc = refs[7:10]
    width, latents = w_ref.shape[1:]
    acc[...] = jnp.broadcast_to(b_ref[...], acc.shape)
    for cols in sixths(width):
        acc[...] += dot(stacked(pieces, cols), w_ref[0, cols, :])
    lane = lax.broadcasted_iota(jnp.int32, (CAP, BLK), 1)
    for r in range(SIDE):
        rows = pl.ds(r * CAP, CAP)
        tail = pieces[r][:, pl.ds(width, BLK)]
        codes_ref[rows, pl.ds(latents, BLK)] = jnp.where(lane == FLAG_AT, flag_ref[...].astype(F32), tail.astype(F32)).astype(BF16)
        here = jnp.where(lane < slots, tail.astype(F32), 0.0)
        for b in range(latents // BLK):
            number = (s[0] * (latents // BLK) + (b + 1)).astype(F32)
            active = jnp.max(jnp.where(here == number, 1.0, 0.0), axis=1, keepdims=True)
            pre = acc[rows, pl.ds(b * BLK, BLK)]
            decay = jnp.exp(-jnp.abs(pre))
            soft = jnp.maximum(pre, 0.0) + jnp.log1p(decay)
            slope = jnp.where(pre >= 0, 1.0, decay) / (1.0 + decay)
            codes_ref[rows, pl.ds(b * BLK, BLK)] = (active * soft).astype(BF16)
            gate_ref[rows, pl.ds(b * BLK, BLK)] = active * slope


def encode(scalars, pieces, w_enc, b_enc, flag, slots):
    latents = w_enc.shape[2]
    outs = [((ROWS, latents + BLK), BF16), ((ROWS, latents), F32)]
    kernel = functools.partial(encode_kernel, slots)
    return call(kernel, "encode", scalars, [*pieces, w_enc, b_enc, flag], outs, [pltpu.VMEM((ROWS, latents), F32)])


def decode_self_kernel(slots, s, codes_ref, w_ref, sum_ref, slot_ref):
    latents, width = w_ref.shape[1:]
    for cols in sixths(width):
        sum_ref[:, cols] = dot(codes_ref[:, pl.ds(0, latents)], w_ref[0, :, cols])
    lane = lax.broadcasted_iota(jnp.int32, (CAP, BLK), 1)
    for r in range(SIDE):
        rows = pl.ds(r * CAP, CAP)
        here = jnp.where(lane < slots, codes_ref[rows, pl.ds(latents, BLK)].astype(F32), 0.0)
        picked = [jnp.zeros((CAP, BLK), F32) for _ in range(slots)]
        for b in range(latents // BLK):
            number = (s[0] * (latents // BLK) + (b + 1)).astype(F32)
            wide = codes_ref[rows, pl.ds(b * BLK, BLK)].astype(F32)
            for k in range(slots):
                picked[k] = jnp.where(here[:, k : k + 1] == number, wide, picked[k])
        for k in range(slots):
            slot_ref[rows, pl.ds(k * BLK, BLK)] = picked[k].astype(BF16)


def decode_self(scalars, codes, w_self, slots):
    outs = [((ROWS, w_self.shape[2]), F32), ((ROWS, slots * BLK), BF16)]
    return call(functools.partial(decode_self_kernel, slots), "decode_self", scalars, [codes, w_self], outs)


def decode_kernel(s, own_ref, other_ref, sum_ref, cross_first_ref, cross_ref, slot_ref, *refs):
    outs, source_ref, match_ref = refs[:4], refs[4], refs[5]
    latents, half = cross_ref.shape
    width = 2 * half
    first = s[1] == 0
    own, other = own_ref[:, pl.ds(latents, BLK)], other_ref[:, pl.ds(latents, BLK)]
    one, zero = jnp.where(first, other, own), jnp.where(first, own, other)
    lane = lax.broadcasted_iota(jnp.int32, (8, BLK), 1)
    row = lax.broadcasted_iota(jnp.int32, (8, BLK), 0)
    take = jnp.where(lane == row + OWNER_AT, 1.0, 0.0).astype(BF16)

    def matched(cols, rows):
        numbers = contract_cols(take, rows)
        owner = cols[:, OWNER_AT : OWNER_AT + 1].astype(F32)
        place = cols[:, PLACE_AT : PLACE_AT + 1].astype(F32)
        hit = (owner == numbers[0:1]) & (place == numbers[1:2]) & (owner > 0.5)
        return jnp.where(hit, 1.0, 0.0).astype(BF16)

    match_ref[...] = matched(zero, one)
    codes = jnp.where(first, own_ref[:, pl.ds(0, latents)], other_ref[:, pl.ds(0, latents)])
    source_ref[...] = dot(matched(one, zero), codes).astype(BF16)
    slots = slot_ref.shape[1]
    flag = (own + other).astype(F32)[:CAP, FLAG_AT : FLAG_AT + 1]
    flag = jnp.broadcast_to(flag, (CAP, BLK)).astype(BF16)
    for r in range(SIDE):
        outs[r][:, pl.ds(width, slots)] = slot_ref[pl.ds(r * CAP, CAP), :]
        outs[r][:, pl.ds(width + slots, BLK)] = flag

    def put(cols, value):
        value = value.astype(BF16)
        for r in range(SIDE):
            outs[r][:, cols] = value[r * CAP : (r + 1) * CAP]

    @pl.when(first)
    def _():
        for cols in sixths(width):
            put(cols, sum_ref[:, cols])

    @pl.when(jnp.logical_not(first))
    def _():
        for cols in sixths(width):
            cross = cross_first_ref[:, cols] if cols.start < half else cross_ref[:, pl.ds(cols.start - half, cols.size)]
            put(cols, sum_ref[:, cols] + dot(source_ref[...], cross))


def decode(scalars, own, other, self_sum, w_cross_first, w_cross, slotted):
    latents, half = w_cross.shape
    wide = 2 * half + slotted.shape[1] + BLK
    outs = [((CAP, wide), BF16)] * 4 + [((ROWS, latents), BF16), ((ROWS, ROWS), BF16)]
    ins = [own, other, self_sum, w_cross_first, w_cross, slotted]
    *sums, source, match = call(decode_kernel, "decode", scalars, ins, outs)
    return sums, source, match


def spread_kernel(s, spread_ref, *refs):
    pieces, outs = refs[:4], refs[4:]
    width = pieces[0].shape[1]
    step = 9 * BLK
    for at in range(0, width, step):
        cols = pl.ds(at, min(step, width - at))
        total = dot(spread_ref[...], stacked(pieces, cols)).astype(BF16)
        for m in range(SIDE):
            outs[m][:, cols] = total[m * LINE : (m + 1) * LINE]
    tail = pl.ds(width - BLK, BLK)
    flag = sum(p[0:16, tail].astype(F32) for p in pieces)
    flag = jnp.concatenate([flag, flag], axis=0).astype(BF16)
    for m in range(SIDE):
        outs[m][:, tail] = flag


def spread_sum(scalars, spread, pieces):
    outs = [((LINE, pieces[0].shape[1]), BF16)] * 4
    return call(spread_kernel, "spread", scalars, [spread, *pieces], outs)


def compact_kernel(s, pick_ref, *refs):
    pieces, outs = refs[:4], refs[4:]
    for cols in sixths(pieces[0].shape[1]):
        chosen = dot(pick_ref[...], stacked(pieces, cols)).astype(BF16)
        for r in range(SIDE):
            outs[r][:, cols] = chosen[r * CAP : (r + 1) * CAP]


def compact(scalars, pick, pieces):
    outs = [((CAP, pieces[0].shape[1]), BF16)] * 4
    return call(compact_kernel, "compact", scalars, [pick, *pieces], outs)


def cross_kernel(s, match_ref, cross_first_ref, cross_ref, *refs):
    pieces, out_ref, acc = refs[:4], refs[4], refs[5]
    latents, half = cross_ref.shape

    @pl.when(s[1] != 0)
    def _():
        acc[...] = jnp.zeros(acc.shape, F32)
        for cols in sixths(2 * half):
            err = stacked(pieces, cols)
            if cols.start < half:
                out_ref[:, cols] = err
                acc[...] += contract_cols(err, cross_first_ref[:, cols])
            else:
                acc[...] += contract_cols(err, cross_ref[:, pl.ds(cols.start - half, cols.size)])
        value = acc[...]
        high = value.astype(BF16)
        rest = (value - high.astype(F32)).astype(BF16)
        turned = dot(match_ref[...], high) + dot(match_ref[...], rest)
        high = turned.astype(BF16)
        out_ref[:, pl.ds(half, latents)] = high
        out_ref[:, pl.ds(half + latents, latents)] = (turned - high.astype(F32)).astype(BF16)


def cross_back(scalars, match, pieces, w_cross_first, w_cross):
    latents, half = w_cross.shape
    outs = [((ROWS, half + 2 * latents), BF16)]
    ins = [match, w_cross_first, w_cross, *pieces]
    return call(cross_kernel, "cross_back", scalars, ins, outs, [pltpu.VMEM((ROWS, latents), F32)])[0]


def self_kernel(s, codes_ref, w_ref, *refs):
    pieces, term_ref, grad_ref, turned, grad, sems = refs[:4], *refs[4:]
    latents, width = w_ref.shape[1:]
    writer = Writer(sems)
    turned[...] = codes_ref[:, pl.ds(0, latents)].T
    term_ref[...] = jnp.zeros(term_ref.shape, F32)
    for cols in sixths(width):
        err = stacked(pieces, cols)
        grad[:, cols] = dot(turned[...], err).astype(BF16)
        writer.write(grad.at[:, cols], grad_ref.at[0, :, cols])
        term_ref[...] += contract_cols(err, w_ref[0, :, cols])
    writer.finish()


def self_back(scalars, codes, pieces, w_self):
    latents, width = w_self.shape[1:]
    outs = [((ROWS, latents), F32), (w_self.shape, BF16, pltpu.HBM)]
    scratch = [pltpu.VMEM((latents, ROWS), BF16), pltpu.VMEM((latents, width), BF16), pltpu.SemaphoreType.DMA((6,))]
    return call(self_kernel, "self_back", scalars, [codes, w_self, *pieces], outs, scratch)


def last_kernel(s, term_ref, gate_ref, source_ref, returned_ref, tail_ref, *refs):
    x, errs = refs[:4], refs[4:8]
    enc_ref, bias_ref, cross_ref, picked_ref, again_ref = refs[8:13]
    dpre, turned, enc, cross, sems = refs[13:]
    width, half = enc.shape[0], cross.shape[1]
    writer = Writer(sems)
    latents = dpre.shape[1]
    again_ref[0] = jnp.where(jnp.max(tail_ref[:, pl.ds(tail_ref.shape[1] - BLK, BLK)]) > 0.5, 1, 0)
    back = [returned_ref[:, pl.ds(at, latents)].astype(F32) for at in (half, half + latents)]
    value = ((term_ref[...] + (back[0] + back[1])) * gate_ref[...]).astype(BF16)
    dpre[...] = value
    bias_ref[...] = jnp.sum(value.astype(F32), axis=0, keepdims=True)
    for cols in sixths(width):
        enc[cols, :] = contract_rows(stacked(x, cols), dpre[...]).astype(BF16)
        writer.write(enc.at[cols, :], enc_ref.at[0, cols, :])
    tokens, slots = tail_ref.shape[0], tail_ref.shape[1] // BLK - 1
    rows = [tail_ref[t : t + 1, pl.ds(k * BLK, BLK)] for t in range(tokens) for k in range(slots)]
    picked_ref[...] = jnp.concatenate(rows, axis=0).astype(BF16)
    turned[...] = source_ref[...].T
    step = half // 3

    @pl.when(s[1] == 0)
    def _():
        for j in range(3):
            cols = pl.ds(j * step, step)
            cross[:, cols] = dot(turned[...], returned_ref[:, cols]).astype(BF16)

    @pl.when(s[1] != 0)
    def _():
        for j in range(3):
            err = stacked(errs, pl.ds(half + j * step, step))
            cross[:, pl.ds(j * step, step)] = dot(turned[...], err).astype(BF16)

    writer.write(cross, cross_ref)
    writer.finish()


def last(scalars, term, gate, source, returned, tail, x, errs):
    latents, half = source.shape[1], returned.shape[1] - 2 * source.shape[1]
    picked = tail.shape[0] * (tail.shape[1] // BLK - 1)
    outs = [((1, 2 * half, latents), BF16, pltpu.HBM), ((1, latents), F32), ((latents, half), BF16, pltpu.HBM)]
    outs += [((picked, BLK), BF16), ((1,), jnp.int32, pltpu.SMEM)]
    scratch = [pltpu.VMEM((ROWS, latents), BF16), pltpu.VMEM((latents, ROWS), BF16)]
    scratch += [pltpu.VMEM((2 * half, latents), BF16), pltpu.VMEM((latents, half), BF16)]
    scratch += [pltpu.SemaphoreType.DMA((7,))]
    ins = [term, gate, source, returned, tail, *x, *errs]
    return call(last_kernel, "last", scalars, ins, outs, scratch)


def reorder(rows, axes):
    shape = (SIDE, SIDE, SIDE, -1, rows.shape[-1])
    return jnp.transpose(rows.reshape(shape), (*axes, 3, 4)).reshape(rows.shape)


def to_second_order(rows):
    return reorder(rows, (2, 0, 1))


def to_first_order(rows):
    return reorder(rows, (1, 2, 0))


def gather_all(rows):
    for axes in (INNER, MIDDLE, OUTER):
        rows = jnp.concatenate(line_gather(rows, axes), axis=0)
    return rows


def reduce_all(rows):
    for axes in (OUTER, MIDDLE, INNER):
        rows = line_reduce(jnp.split(rows, SIDE, axis=0), axes)
    return rows


def dense(inputs, targets, w_enc, b_enc, w_self, w_cross, block_ids, w_cross_first):
    first_layer = lax.axis_index("layer") == 0
    width = inputs.shape[2]
    half = width // 2
    blocks = w_enc.shape[2] // BLK
    slots = block_ids.shape[2]
    tail = jnp.pad(block_ids[0].astype(BF16), ((0, 0), (0, BLK - slots)))
    gathered = gather_all(jnp.concatenate([inputs[0], tail], axis=1))
    x, ids = gathered[:, :width], gathered[:, width : width + slots].astype(jnp.int32)
    own_blocks = lax.axis_index("feat") * blocks + jnp.arange(blocks, dtype=jnp.int32)
    hit = ids[:, :, None] == own_blocks[None, None, :]
    active = jnp.repeat(jnp.any(hit, axis=1), BLK, axis=1).astype(F32)
    pre = dot(x, w_enc[0]) + b_enc[0]
    codes = (active * jax.nn.softplus(pre)).astype(BF16)
    turned = to_second_order(codes)
    earlier = to_second(turned)
    source = jnp.where(first_layer, turned, earlier)
    by_block = codes.reshape(-1, 1, blocks, BLK)
    slotted = jnp.sum(jnp.where(hit[..., None], by_block, 0).astype(F32), axis=2).reshape(-1, slots * BLK)
    w_cross_all = jnp.concatenate([w_cross_first, w_cross], axis=1)
    partial = dot(codes, w_self[0]) + dot(earlier, w_cross_all)
    summed = reduce_all(jnp.concatenate([partial, slotted], axis=1).astype(BF16))
    recon = summed[:, :width]
    picked = summed[:, width:].astype(BF16).reshape(-1, slots, BLK)
    err = gather_all((recon - targets[0].astype(F32)).astype(BF16))
    back = to_first_order(to_first(contract_cols(err, w_cross_all)))
    returned = to_first(err[:, :half])
    term = contract_cols(err, w_self[0])
    grad_self = contract_rows(codes, err).astype(BF16)
    cross_err = jnp.where(first_layer, returned, err[:, half:])
    grad_cross = contract_rows(source, cross_err).astype(BF16)
    code_grads = term + jnp.where(first_layer, back, 0.0)
    pre_grads = (code_grads * active * jax.nn.sigmoid(pre)).astype(BF16)
    grad_enc = contract_rows(x, pre_grads).astype(BF16)
    grad_benc = jnp.sum(pre_grads.astype(F32), axis=0)
    return recon, picked, grad_enc, grad_benc[None], grad_self, grad_cross


def per_device(inputs, targets, w_enc, b_enc, w_self, w_cross, block_ids):
    layer = lax.axis_index("layer")
    shard = lax.axis_index("feat")
    width = inputs.shape[2]
    slots = block_ids.shape[2]
    tokens_dev = inputs.shape[1]

    y, z = shard // (SIDE * SIDE), shard % SIDE
    receivers = [
        jnp.where(layer == 0, shard - z + (z - r) % SIDE, shard + SIDE * SIDE * ((y - r) % SIDE - y))
        for r in AWAY
    ]
    scalars = jnp.stack([shard, layer] + receivers).astype(jnp.int32)

    own_ids, other_ids = (ids[0].astype(BF16) + 1 for ids in (block_ids, swapped(block_ids)))
    owner = jnp.full((tokens_dev, 1), shard + 1).astype(BF16)
    place = jnp.arange(tokens_dev, dtype=jnp.int32)[:, None].astype(BF16)
    spare = jnp.zeros((tokens_dev, BLK - 2 * slots - 2), BF16)
    rows = jnp.concatenate([inputs[0], own_ids, other_ids, owner, place, spare], axis=1)

    line = jnp.concatenate(line_gather(rows, INNER), axis=0)
    chosen, pick, spread, flag = select(scalars, line_gather(line, MIDDLE))
    x = ahead(chosen[0], chosen, OUTER)
    x, half_cross = lax.optimization_barrier((x, w_cross))
    w_cross_first = to_second(half_cross)
    codes, gate = encode(scalars, x, w_enc, b_enc, flag, slots)
    other_codes = swapped(codes)
    self_sum, slotted = decode_self(scalars, codes, w_self, slots)
    sums, source, match = decode(scalars, codes, other_codes, self_sum, w_cross_first, w_cross, slotted)
    sums = behind(sums, OUTER)
    on_line = line_reduce(spread_sum(scalars, spread, sums), MIDDLE)
    summed = line_reduce([on_line[8 * r : 8 * r + 8] for r in range(SIDE)], INNER)
    recon = summed[:, :width]
    tail = summed[:, width:]

    err = (recon - targets[0].astype(F32)).astype(BF16)
    err_line = jnp.concatenate(line_gather(err, INNER), axis=0)
    err_plane = line_gather(err_line, MIDDLE)

    kept = compact(scalars, pick, err_plane)
    errs = ahead(kept[0], kept, OUTER)
    returned = to_first(cross_back(scalars, match, errs, w_cross_first, w_cross))
    term, grad_self = self_back(scalars, codes, errs, w_self)
    grad_enc, grad_benc, grad_cross, picked, again = last(scalars, term, gate, source, returned, tail, x, errs)

    def on_every_row(_):
        results = dense(inputs, targets, w_enc, b_enc, w_self, w_cross, block_ids, w_cross_first)
        recon, picked, grad_enc, grad_benc, grad_self, grad_cross = results
        return jnp.int32(0), recon[None], picked.reshape(-1, BLK), grad_enc[None], grad_benc, grad_self[None], grad_cross

    results = (again[0], recon[None], picked, grad_enc, grad_benc, grad_self, grad_cross)
    _, recon, picked, *grads = lax.while_loop(lambda carried: carried[0] > 0, on_every_row, results)
    return recon, picked.reshape(1, tokens_dev, slots, BLK), *grads


def solution(mesh):
    placed = (
        P("layer", "feat", None),
        P("layer", "feat", None),
        P("layer", None, "feat"),
        P("layer", "feat"),
        P("layer", "feat", None),
        P("feat", "layer"),
        P("layer", "feat", None),
    )
    return jax.shard_map(
        per_device,
        mesh=mesh,
        in_specs=placed,
        out_specs=(
            P("layer", "feat", None),
            P("layer", "feat", None, None),
            P("layer", None, "feat"),
            P("layer", "feat"),
            P("layer", "feat", None),
            P("feat", "layer"),
        ),
        check_vma=False,
    )
```

```python
import functools

import jax
import jax.numpy as jnp
from jax import lax
from jax.experimental import pallas as pl
from jax.experimental.pallas import tpu as pltpu
from jax.sharding import PartitionSpec as P

BLK = 128
SIDE = 4
LINE = 32
PLANE = 128
CAP = 64
ROWS = SIDE * CAP
AWAY = (0, 2, 1, 3)
STEPS = {"y": (1, 0, 0), "x": (0, 1, 0), "z": (0, 0, 1)}
F32, BF16 = jnp.float32, jnp.bfloat16

OUTER = ("z", "y")
MIDDLE = ("x", "z")
INNER = ("y", "x")

PARAMS = pltpu.CompilerParams(vmem_limit_bytes=20 * 2**20)


def route(axes, distance):
    pairs = []
    for core, axis in enumerate(axes):
        step = STEPS[axis]
        for y in range(SIDE):
            for x in range(SIDE):
                for z in range(SIDE):
                    there = [(c + distance * s) % SIDE for c, s in zip((y, x, z), step)]
                    base = core * SIDE**3
                    pairs.append(
                        (base + (y * SIDE + x) * SIDE + z, base + (there[0] * SIDE + there[1]) * SIDE + there[2])
                    )
    return pairs


def send(block, axes, distance):
    return lax.ppermute(block, ("layer", "feat"), route(axes, distance))


def ahead(block, pieces, axes):
    return [block] + [send(pieces[r], axes, -AWAY[r]) for r in (1, 2, 3)]


def behind(pieces, axes):
    return [pieces[0]] + [send(pieces[r], axes, AWAY[r]) for r in (1, 2, 3)]


def to_second(block):
    return lax.ppermute(block, "layer", [(0, 1)])


def to_first(block):
    return lax.ppermute(block, "layer", [(1, 0)])


def swapped(block):
    return lax.ppermute(block, "layer", [(0, 1), (1, 0)])


def line_gather(block, axes):
    return ahead(block, [block] * SIDE, axes)


def line_reduce(terms, axes):
    terms = behind([terms[0]] + [term.astype(BF16) for term in terms[1:]], axes)
    return sum(term.astype(F32) for term in terms)


def contract_rows(left, right):
    return lax.dot_general(left, right, (((0,), (0,)), ((), ())), preferred_element_type=F32)


def contract_cols(left, right):
    return lax.dot_general(left, right, (((1,), (1,)), ((), ())), preferred_element_type=F32)


def dot(left, right):
    return jnp.dot(left, right, preferred_element_type=F32)


def call(kernel, name, scalars, ins, outs, scratch=()):
    size = sum(a.size * a.dtype.itemsize for a in ins)
    vmem, smem = pl.BlockSpec(memory_space=pltpu.VMEM), pl.BlockSpec(memory_space=pltpu.SMEM)
    return pl.pallas_call(
        kernel,
        in_specs=[smem] + [vmem] * len(ins),
        out_specs=[pl.BlockSpec(memory_space=out[2]) if len(out) > 2 else vmem for out in outs],
        out_shape=[jax.ShapeDtypeStruct(out[0], out[1]) for out in outs],
        scratch_shapes=list(scratch),
        compiler_params=PARAMS,
        cost_estimate=pl.CostEstimate(flops=2**31, bytes_accessed=size, transcendentals=0),
        name=name,
    )(scalars, *ins)


class Writer:
    def __init__(self, sems):
        self.sems, self.started = sems, []

    def write(self, source, target):
        copy = pltpu.make_async_copy(source, target, self.sems.at[len(self.started)])
        copy.start()
        self.started.append(copy)

    def finish(self):
        for copy in self.started:
            copy.wait()


def sixths(width):
    step = width // 6
    return [pl.ds(j * step, step) for j in range(6)]


def stacked(pieces, cols):
    return jnp.concatenate([p[:, cols] for p in pieces], axis=0)


OWNER_AT, PLACE_AT, FLAG_AT = 16, 17, 18
TOO_MANY = -1e30


def select_kernel(s, *refs):
    pieces, outs = refs[:4], refs[4:8]
    pick_ref, spread_ref, flag_ref = refs[8:11]
    width = pieces[0].shape[1]
    tail = jnp.concatenate([p[:, width - BLK :] for p in pieces], axis=0).astype(F32)
    lane = lax.broadcasted_iota(jnp.int32, (PLANE, BLK), 1)
    row = lax.broadcasted_iota(jnp.int32, (PLANE, BLK), 0)
    numbers = jnp.where(lane < OWNER_AT, tail, 0.0)
    needs = jnp.zeros((PLANE, BLK), F32)
    for r in range(SIDE):
        low = (s[2 + r] * 4).astype(F32)
        inside = jnp.where((numbers > low + 0.5) & (numbers < low + 4.5), 1.0, 0.0)
        needs = jnp.where(lane == r, jnp.max(inside, axis=1, keepdims=True), needs)
    needs = needs.astype(BF16)
    upto = jnp.where(row <= lane, 1.0, 0.0).astype(BF16)
    same = jnp.where(row == lane, 1.0, 0.0).astype(BF16)
    down = jnp.where(lane <= row, 1.0, 0.0).astype(BF16)
    count_rows = contract_rows(needs, upto)
    need_rows = contract_rows(needs, same)
    count_cols = dot(down, needs)
    need_cols = needs.astype(F32)
    place = lax.broadcasted_iota(jnp.int32, (CAP, BLK), 0).astype(F32) + 1.0
    for r in range(SIDE):
        hit = (count_rows[r : r + 1, :] == place) & (need_rows[r : r + 1, :] > 0.5)
        pick_ref[pl.ds(r * CAP, CAP), :] = jnp.where(hit, 1.0, 0.0).astype(BF16)
    half = lane < CAP
    place = jnp.where(half, lane, lane - CAP).astype(F32) + 1.0
    for pair in range(2):
        a, b = 2 * pair, 2 * pair + 1
        count = jnp.where(half, count_cols[:, a : a + 1], count_cols[:, b : b + 1])
        need = jnp.where(half, need_cols[:, a : a + 1], need_cols[:, b : b + 1])
        hit = (count == place) & (need > 0.5)
        spread_ref[:, pl.ds(pair * BLK, BLK)] = jnp.where(hit, 1.0, 0.0).astype(BF16)
    most = jnp.max(jnp.max(count_cols, axis=1, keepdims=True), axis=0, keepdims=True)
    flag_ref[...] = jnp.broadcast_to(jnp.where(most > CAP + 0.5, 1.0, 0.0), flag_ref.shape).astype(BF16)
    pick = pick_ref[...]
    for at in range(0, width, 1024):
        cols = pl.ds(at, min(1024, width - at))
        plane = jnp.concatenate([p[:, cols] for p in pieces], axis=0)
        chosen = dot(pick, plane).astype(BF16)
        for r in range(SIDE):
            outs[r][:, cols] = chosen[r * CAP : (r + 1) * CAP]


def select(scalars, pieces):
    width = pieces[0].shape[1]
    outs = [((CAP, width), BF16)] * 4 + [((ROWS, PLANE), BF16), ((PLANE, ROWS), BF16), ((CAP, BLK), BF16)]
    *chosen, pick, spread, flag = call(select_kernel, "select", scalars, pieces, outs)
    return chosen, pick, spread, flag


def encode_kernel(slots, s, *refs):
    pieces, w_ref, b_ref, flag_ref = refs[:4], *refs[4:7]
    codes_ref, gate_ref, acc = refs[7:10]
    width, latents = w_ref.shape[1:]
    acc[...] = jnp.broadcast_to(b_ref[...], acc.shape)
    for cols in sixths(width):
        acc[...] += dot(stacked(pieces, cols), w_ref[0, cols, :])
    lane = lax.broadcasted_iota(jnp.int32, (CAP, BLK), 1)
    for r in range(SIDE):
        rows = pl.ds(r * CAP, CAP)
        tail = pieces[r][:, pl.ds(width, BLK)]
        codes_ref[rows, pl.ds(latents, BLK)] = jnp.where(lane == FLAG_AT, flag_ref[...].astype(F32), tail.astype(F32)).astype(BF16)
        here = jnp.where(lane < slots, tail.astype(F32), 0.0)
        for b in range(latents // BLK):
            number = (s[0] * (latents // BLK) + (b + 1)).astype(F32)
            active = jnp.max(jnp.where(here == number, 1.0, 0.0), axis=1, keepdims=True)
            pre = acc[rows, pl.ds(b * BLK, BLK)]
            decay = jnp.exp(-jnp.abs(pre))
            soft = jnp.maximum(pre, 0.0) + jnp.log1p(decay)
            slope = jnp.where(pre >= 0, 1.0, decay) / (1.0 + decay)
            codes_ref[rows, pl.ds(b * BLK, BLK)] = (active * soft).astype(BF16)
            gate_ref[rows, pl.ds(b * BLK, BLK)] = active * slope


def encode(scalars, pieces, w_enc, b_enc, flag, slots):
    latents = w_enc.shape[2]
    outs = [((ROWS, latents + BLK), BF16), ((ROWS, latents), F32)]
    kernel = functools.partial(encode_kernel, slots)
    return call(kernel, "encode", scalars, [*pieces, w_enc, b_enc, flag], outs, [pltpu.VMEM((ROWS, latents), F32)])


def decode_self_kernel(slots, s, codes_ref, w_ref, sum_ref, slot_ref):
    latents, width = w_ref.shape[1:]
    for cols in sixths(width):
        sum_ref[:, cols] = dot(codes_ref[:, pl.ds(0, latents)], w_ref[0, :, cols])
    lane = lax.broadcasted_iota(jnp.int32, (CAP, BLK), 1)
    for r in range(SIDE):
        rows = pl.ds(r * CAP, CAP)
        here = jnp.where(lane < slots, codes_ref[rows, pl.ds(latents, BLK)].astype(F32), 0.0)
        picked = [jnp.zeros((CAP, BLK), F32) for _ in range(slots)]
        for b in range(latents // BLK):
            number = (s[0] * (latents // BLK) + (b + 1)).astype(F32)
            wide = codes_ref[rows, pl.ds(b * BLK, BLK)].astype(F32)
            for k in range(slots):
                picked[k] = jnp.where(here[:, k : k + 1] == number, wide, picked[k])
        for k in range(slots):
            slot_ref[rows, pl.ds(k * BLK, BLK)] = picked[k].astype(BF16)


def decode_self(scalars, codes, w_self, slots):
    outs = [((ROWS, w_self.shape[2]), F32), ((ROWS, slots * BLK), BF16)]
    return call(functools.partial(decode_self_kernel, slots), "decode_self", scalars, [codes, w_self], outs)


def decode_kernel(s, own_ref, other_ref, sum_ref, cross_first_ref, cross_ref, slot_ref, *refs):
    outs, source_ref, match_ref = refs[:4], refs[4], refs[5]
    latents, half = cross_ref.shape
    width = 2 * half
    first = s[1] == 0
    own, other = own_ref[:, pl.ds(latents, BLK)], other_ref[:, pl.ds(latents, BLK)]
    one, zero = jnp.where(first, other, own), jnp.where(first, own, other)
    lane = lax.broadcasted_iota(jnp.int32, (8, BLK), 1)
    row = lax.broadcasted_iota(jnp.int32, (8, BLK), 0)
    take = jnp.where(lane == row + OWNER_AT, 1.0, 0.0).astype(BF16)

    def matched(cols, rows):
        numbers = contract_cols(take, rows)
        owner = cols[:, OWNER_AT : OWNER_AT + 1].astype(F32)
        place = cols[:, PLACE_AT : PLACE_AT + 1].astype(F32)
        hit = (owner == numbers[0:1]) & (place == numbers[1:2]) & (owner > 0.5)
        return jnp.where(hit, 1.0, 0.0).astype(BF16)

    match_ref[...] = matched(zero, one)
    codes = jnp.where(first, own_ref[:, pl.ds(0, latents)], other_ref[:, pl.ds(0, latents)])
    source_ref[...] = dot(matched(one, zero), codes).astype(BF16)
    slots = slot_ref.shape[1]
    flag = (own + other).astype(F32)[:CAP, FLAG_AT : FLAG_AT + 1]
    flag = jnp.broadcast_to(flag, (CAP, slots)) > 0.5
    for r in range(SIDE):
        slotted = jnp.where(flag, TOO_MANY, slot_ref[pl.ds(r * CAP, CAP), :].astype(F32))
        outs[r][:, pl.ds(width, slots)] = slotted.astype(BF16)

    def put(cols, value):
        value = value.astype(BF16)
        for r in range(SIDE):
            outs[r][:, cols] = value[r * CAP : (r + 1) * CAP]

    @pl.when(first)
    def _():
        for cols in sixths(width):
            put(cols, sum_ref[:, cols])

    @pl.when(jnp.logical_not(first))
    def _():
        for cols in sixths(width):
            cross = cross_first_ref[:, cols] if cols.start < half else cross_ref[:, pl.ds(cols.start - half, cols.size)]
            put(cols, sum_ref[:, cols] + dot(source_ref[...], cross))


def decode(scalars, own, other, self_sum, w_cross_first, w_cross, slotted):
    latents, half = w_cross.shape
    wide = 2 * half + slotted.shape[1]
    outs = [((CAP, wide), BF16)] * 4 + [((ROWS, latents), BF16), ((ROWS, ROWS), BF16)]
    ins = [own, other, self_sum, w_cross_first, w_cross, slotted]
    *sums, source, match = call(decode_kernel, "decode", scalars, ins, outs)
    return sums, source, match


def spread_kernel(main, s, spread_ref, *refs):
    pieces, outs = refs[:4], refs[4:]
    width = pieces[0].shape[1]
    step = 9 * BLK
    for at in range(0, width, step):
        cols = pl.ds(at, min(step, width - at))
        total = dot(spread_ref[...], stacked(pieces, cols)).astype(BF16)
        for m in range(SIDE):
            outs[m][:, cols] = total[m * LINE : (m + 1) * LINE]
    least = jnp.min(sum(p[0:16, pl.ds(main, BLK)].astype(F32) for p in pieces))

    @pl.when(least < -0.5)
    def _():
        for m in range(SIDE):
            outs[m][:, pl.ds(main, width - main)] = jnp.full((LINE, width - main), TOO_MANY, F32).astype(BF16)


def spread_sum(scalars, spread, pieces, main):
    outs = [((LINE, pieces[0].shape[1]), BF16)] * 4
    return call(functools.partial(spread_kernel, main), "spread", scalars, [spread, *pieces], outs)


def line_kernel(s, *refs):
    pieces, targets_ref, exact_ref, sents = refs[:4], refs[4], refs[5], refs[6:]
    tokens, width = targets_ref.shape[1:]
    for cols in sixths(width):
        total = sum(p[:, cols].astype(F32) for p in pieces)
        own = total[:tokens] - targets_ref[0, :, cols].astype(F32)
        total = jnp.concatenate([own, total[tokens:]], axis=0)
        exact_ref[:, cols] = total
        for sent in sents:
            sent[:, cols] = total.astype(BF16)
    slots = exact_ref.shape[1] - width
    quarter = slots // SIDE
    total = sum(p[:, pl.ds(width, slots)].astype(F32) for p in pieces)
    exact_ref[:, pl.ds(width, slots)] = total
    for r in (1, 2, 3):
        i = AWAY.index(-AWAY[r] % SIDE)
        rows = total[tokens * i : tokens * (i + 1)]
        folded = jnp.concatenate([rows[:, quarter * c : quarter * (c + 1)] for c in range(SIDE)], axis=0)
        sents[r - 1][:, pl.ds(width, quarter)] = folded.astype(BF16)


def line_terms(scalars, pieces, targets):
    rows, columns = pieces[0].shape
    width = targets.shape[2]
    outs = [((rows, columns), F32)] + [((rows, width + (columns - width) // SIDE), BF16)] * 3
    exact, *sents = call(line_kernel, "line", scalars, [*pieces, targets], outs)
    return exact, [exact, *sents]


def settle_kernel(s, exact_ref, *refs):
    came, targets_ref, err_ref, recon_ref, tail_ref = refs[:3], *refs[3:]
    tokens, width = targets_ref.shape[1:]
    for cols in sixths(width):
        total = exact_ref[:, cols]
        for r in (1, 2, 3):
            value = came[r - 1][:, cols].astype(F32)
            order = [AWAY.index((AWAY[j] - AWAY[r]) % SIDE) for j in range(SIDE)]
            total += jnp.concatenate([value[tokens * i : tokens * (i + 1)] for i in order], axis=0)
        err_ref[:, cols] = total.astype(BF16)
        recon_ref[0, :, cols] = total[:tokens] + targets_ref[0, :, cols].astype(F32)
    slots = tail_ref.shape[1]
    tail = exact_ref[0:tokens, pl.ds(width, slots)]
    for r in (1, 2, 3):
        value = came[r - 1][:, pl.ds(width, slots // SIDE)].astype(F32)
        tail += jnp.concatenate([value[tokens * c : tokens * (c + 1)] for c in range(SIDE)], axis=1)
    tail_ref[...] = tail


def settle(scalars, exact, came, targets):
    rows, columns = exact.shape
    tokens, width = targets.shape[1:]
    outs = [((rows, width), BF16), ((1, tokens, width), F32), ((tokens, columns - width), F32)]
    return call(settle_kernel, "settle", scalars, [exact, *came, targets], outs)


def compact_kernel(s, pick_ref, *refs):
    pieces, outs = refs[:4], refs[4:]
    for cols in sixths(pieces[0].shape[1]):
        chosen = dot(pick_ref[...], stacked(pieces, cols)).astype(BF16)
        for r in range(SIDE):
            outs[r][:, cols] = chosen[r * CAP : (r + 1) * CAP]


def compact(scalars, pick, pieces):
    outs = [((CAP, pieces[0].shape[1]), BF16)] * 4
    return call(compact_kernel, "compact", scalars, [pick, *pieces], outs)


def cross_kernel(s, match_ref, cross_first_ref, cross_ref, *refs):
    pieces, out_ref, acc = refs[:4], refs[4], refs[5]
    latents, half = cross_ref.shape

    @pl.when(s[1] != 0)
    def _():
        acc[...] = jnp.zeros(acc.shape, F32)
        for cols in sixths(2 * half):
            err = stacked(pieces, cols)
            if cols.start < half:
                out_ref[:, cols] = err
                acc[...] += contract_cols(err, cross_first_ref[:, cols])
            else:
                acc[...] += contract_cols(err, cross_ref[:, pl.ds(cols.start - half, cols.size)])
        value = acc[...]
        high = value.astype(BF16)
        rest = (value - high.astype(F32)).astype(BF16)
        turned = dot(match_ref[...], high) + dot(match_ref[...], rest)
        high = turned.astype(BF16)
        out_ref[:, pl.ds(half, latents)] = high
        out_ref[:, pl.ds(half + latents, latents)] = (turned - high.astype(F32)).astype(BF16)


def cross_back(scalars, match, pieces, w_cross_first, w_cross):
    latents, half = w_cross.shape
    outs = [((ROWS, half + 2 * latents), BF16)]
    ins = [match, w_cross_first, w_cross, *pieces]
    return call(cross_kernel, "cross_back", scalars, ins, outs, [pltpu.VMEM((ROWS, latents), F32)])[0]


def self_kernel(s, codes_ref, w_ref, *refs):
    pieces, term_ref, grad_ref, turned, grad, sems = refs[:4], *refs[4:]
    latents, width = w_ref.shape[1:]
    writer = Writer(sems)
    turned[...] = codes_ref[:, pl.ds(0, latents)].T
    term_ref[...] = jnp.zeros(term_ref.shape, F32)
    for cols in sixths(width):
        err = stacked(pieces, cols)
        grad[:, cols] = dot(turned[...], err).astype(BF16)
        writer.write(grad.at[:, cols], grad_ref.at[0, :, cols])
        term_ref[...] += contract_cols(err, w_ref[0, :, cols])
    writer.finish()


def self_back(scalars, codes, pieces, w_self):
    latents, width = w_self.shape[1:]
    outs = [((ROWS, latents), F32), (w_self.shape, BF16, pltpu.HBM)]
    scratch = [pltpu.VMEM((latents, ROWS), BF16), pltpu.VMEM((latents, width), BF16), pltpu.SemaphoreType.DMA((6,))]
    return call(self_kernel, "self_back", scalars, [codes, w_self, *pieces], outs, scratch)


def last_kernel(s, term_ref, gate_ref, source_ref, returned_ref, tail_ref, *refs):
    x, errs = refs[:4], refs[4:8]
    enc_ref, bias_ref, cross_ref, picked_ref, again_ref = refs[8:13]
    dpre, turned, enc, cross, sems = refs[13:]
    width, half = enc.shape[0], cross.shape[1]
    writer = Writer(sems)
    latents = dpre.shape[1]
    again_ref[0] = jnp.where(jnp.min(tail_ref[...]) < -0.5, 1, 0)
    back = [returned_ref[:, pl.ds(at, latents)].astype(F32) for at in (half, half + latents)]
    value = ((term_ref[...] + (back[0] + back[1])) * gate_ref[...]).astype(BF16)
    dpre[...] = value
    bias_ref[...] = jnp.sum(value.astype(F32), axis=0, keepdims=True)
    for cols in sixths(width):
        enc[cols, :] = contract_rows(stacked(x, cols), dpre[...]).astype(BF16)
        writer.write(enc.at[cols, :], enc_ref.at[0, cols, :])
    tokens, slots = tail_ref.shape[0], tail_ref.shape[1] // BLK
    rows = [tail_ref[t : t + 1, pl.ds(k * BLK, BLK)] for t in range(tokens) for k in range(slots)]
    picked_ref[...] = jnp.concatenate(rows, axis=0).astype(BF16)
    turned[...] = source_ref[...].T
    step = half // 3
    for j in range(3):
        cols = pl.ds(j * step, step)

        @pl.when(s[1] == 0)
        def _():
            cross[:, cols] = dot(turned[...], returned_ref[:, cols]).astype(BF16)

        @pl.when(s[1] != 0)
        def _():
            err = stacked(errs, pl.ds(half + cols.start, step))
            cross[:, cols] = dot(turned[...], err).astype(BF16)

        writer.write(cross.at[:, cols], cross_ref.at[:, cols])
    writer.finish()


def last(scalars, term, gate, source, returned, tail, x, errs):
    latents, half = source.shape[1], returned.shape[1] - 2 * source.shape[1]
    picked = tail.shape[0] * tail.shape[1] // BLK
    outs = [((1, 2 * half, latents), BF16, pltpu.HBM), ((1, latents), F32), ((latents, half), BF16, pltpu.HBM)]
    outs += [((picked, BLK), BF16), ((1,), jnp.int32, pltpu.SMEM)]
    scratch = [pltpu.VMEM((ROWS, latents), BF16), pltpu.VMEM((latents, ROWS), BF16)]
    scratch += [pltpu.VMEM((2 * half, latents), BF16), pltpu.VMEM((latents, half), BF16)]
    scratch += [pltpu.SemaphoreType.DMA((9,))]
    ins = [term, gate, source, returned, tail, *x, *errs]
    return call(last_kernel, "last", scalars, ins, outs, scratch)


def reorder(rows, axes):
    shape = (SIDE, SIDE, SIDE, -1, rows.shape[-1])
    return jnp.transpose(rows.reshape(shape), (*axes, 3, 4)).reshape(rows.shape)


def to_second_order(rows):
    return reorder(rows, (2, 0, 1))


def to_first_order(rows):
    return reorder(rows, (1, 2, 0))


def gather_all(rows):
    for axes in (INNER, MIDDLE, OUTER):
        rows = jnp.concatenate(line_gather(rows, axes), axis=0)
    return rows


def reduce_all(rows):
    for axes in (OUTER, MIDDLE, INNER):
        rows = line_reduce(jnp.split(rows, SIDE, axis=0), axes)
    return rows


def dense(inputs, targets, w_enc, b_enc, w_self, w_cross, block_ids, w_cross_first):
    first_layer = lax.axis_index("layer") == 0
    width = inputs.shape[2]
    half = width // 2
    blocks = w_enc.shape[2] // BLK
    slots = block_ids.shape[2]
    tail = jnp.pad(block_ids[0].astype(BF16), ((0, 0), (0, BLK - slots)))
    gathered = gather_all(jnp.concatenate([inputs[0], tail], axis=1))
    x, ids = gathered[:, :width], gathered[:, width : width + slots].astype(jnp.int32)
    own_blocks = lax.axis_index("feat") * blocks + jnp.arange(blocks, dtype=jnp.int32)
    hit = ids[:, :, None] == own_blocks[None, None, :]
    active = jnp.repeat(jnp.any(hit, axis=1), BLK, axis=1).astype(F32)
    pre = dot(x, w_enc[0]) + b_enc[0]
    codes = (active * jax.nn.softplus(pre)).astype(BF16)
    turned = to_second_order(codes)
    earlier = to_second(turned)
    source = jnp.where(first_layer, turned, earlier)
    by_block = codes.reshape(-1, 1, blocks, BLK)
    slotted = jnp.sum(jnp.where(hit[..., None], by_block, 0).astype(F32), axis=2).reshape(-1, slots * BLK)
    w_cross_all = jnp.concatenate([w_cross_first, w_cross], axis=1)
    partial = dot(codes, w_self[0]) + dot(earlier, w_cross_all)
    summed = reduce_all(jnp.concatenate([partial, slotted], axis=1).astype(BF16))
    recon = summed[:, :width]
    picked = summed[:, width:].astype(BF16).reshape(-1, slots, BLK)
    err = gather_all((recon - targets[0].astype(F32)).astype(BF16))
    back = to_first_order(to_first(contract_cols(err, w_cross_all)))
    returned = to_first(err[:, :half])
    term = contract_cols(err, w_self[0])
    grad_self = contract_rows(codes, err).astype(BF16)
    cross_err = jnp.where(first_layer, returned, err[:, half:])
    grad_cross = contract_rows(source, cross_err).astype(BF16)
    code_grads = term + jnp.where(first_layer, back, 0.0)
    pre_grads = (code_grads * active * jax.nn.sigmoid(pre)).astype(BF16)
    grad_enc = contract_rows(x, pre_grads).astype(BF16)
    grad_benc = jnp.sum(pre_grads.astype(F32), axis=0)
    return recon, picked, grad_enc, grad_benc[None], grad_self, grad_cross


def per_device(inputs, targets, w_enc, b_enc, w_self, w_cross, block_ids):
    layer = lax.axis_index("layer")
    shard = lax.axis_index("feat")
    width = inputs.shape[2]
    slots = block_ids.shape[2]
    tokens_dev = inputs.shape[1]

    y, z = shard // (SIDE * SIDE), shard % SIDE
    receivers = [
        jnp.where(layer == 0, shard - z + (z - r) % SIDE, shard + SIDE * SIDE * ((y - r) % SIDE - y))
        for r in AWAY
    ]
    scalars = jnp.stack([shard, layer] + receivers).astype(jnp.int32)

    own_ids, other_ids = (ids[0].astype(BF16) + 1 for ids in (block_ids, swapped(block_ids)))
    owner = jnp.full((tokens_dev, 1), shard + 1).astype(BF16)
    place = jnp.arange(tokens_dev, dtype=jnp.int32)[:, None].astype(BF16)
    spare = jnp.zeros((tokens_dev, BLK - 2 * slots - 2), BF16)
    rows = jnp.concatenate([inputs[0], own_ids, other_ids, owner, place, spare], axis=1)

    line = jnp.concatenate(line_gather(rows, INNER), axis=0)
    chosen, pick, spread, flag = select(scalars, line_gather(line, MIDDLE))
    x = ahead(chosen[0], chosen, OUTER)
    x, half_cross = lax.optimization_barrier((x, w_cross))
    w_cross_first = to_second(half_cross)
    codes, gate = encode(scalars, x, w_enc, b_enc, flag, slots)
    other_codes = swapped(codes)
    self_sum, slotted = decode_self(scalars, codes, w_self, slots)
    sums, source, match = decode(scalars, codes, other_codes, self_sum, w_cross_first, w_cross, slotted)
    sums = behind(sums, OUTER)
    exact, sents = line_terms(scalars, behind(spread_sum(scalars, spread, sums, width), MIDDLE), targets)
    err_line, recon, tail = settle(scalars, exact, ahead(exact, sents, INNER)[1:], targets)
    err_plane = line_gather(err_line, MIDDLE)
    kept = compact(scalars, pick, err_plane)
    errs = ahead(kept[0], kept, OUTER)
    returned = to_first(cross_back(scalars, match, errs, w_cross_first, w_cross))
    term, grad_self = self_back(scalars, codes, errs, w_self)
    grad_enc, grad_benc, grad_cross, picked, again = last(scalars, term, gate, source, returned, tail, x, errs)

    def on_every_row(_):
        results = dense(inputs, targets, w_enc, b_enc, w_self, w_cross, block_ids, w_cross_first)
        recon, picked, grad_enc, grad_benc, grad_self, grad_cross = results
        return jnp.int32(0), recon[None], picked.reshape(-1, BLK), grad_enc[None], grad_benc, grad_self[None], grad_cross

    results = (again[0], recon, picked, grad_enc, grad_benc, grad_self, grad_cross)
    _, recon, picked, *grads = lax.while_loop(lambda carried: carried[0] > 0, on_every_row, results)
    return recon, picked.reshape(1, tokens_dev, slots, BLK), *grads


def solution(mesh):
    placed = (
        P("layer", "feat", None),
        P("layer", "feat", None),
        P("layer", None, "feat"),
        P("layer", "feat"),
        P("layer", "feat", None),
        P("feat", "layer"),
        P("layer", "feat", None),
    )
    return jax.shard_map(
        per_device,
        mesh=mesh,
        in_specs=placed,
        out_specs=(
            P("layer", "feat", None),
            P("layer", "feat", None, None),
            P("layer", None, "feat"),
            P("layer", "feat"),
            P("layer", "feat", None),
            P("feat", "layer"),
        ),
        check_vma=False,
    )
```

```python
import functools

import jax
import jax.numpy as jnp
from jax import lax
from jax.experimental import pallas as pl
from jax.experimental.pallas import tpu as pltpu
from jax.sharding import PartitionSpec as P

BLK = 128
SIDE = 4
LINE = 32
PLANE = 128
CAP = 64
ROWS = SIDE * CAP
AWAY = (0, 2, 1, 3)
STEPS = {"y": (1, 0, 0), "x": (0, 1, 0), "z": (0, 0, 1)}
F32, BF16 = jnp.float32, jnp.bfloat16

OUTER = ("z", "y")
MIDDLE = ("x", "z")
INNER = ("y", "x")

PARAMS = pltpu.CompilerParams(vmem_limit_bytes=20 * 2**20)


def route(axes, distance):
    pairs = []
    for core, axis in enumerate(axes):
        step = STEPS[axis]
        for y in range(SIDE):
            for x in range(SIDE):
                for z in range(SIDE):
                    there = [(c + distance * s) % SIDE for c, s in zip((y, x, z), step)]
                    base = core * SIDE**3
                    pairs.append(
                        (base + (y * SIDE + x) * SIDE + z, base + (there[0] * SIDE + there[1]) * SIDE + there[2])
                    )
    return pairs


def send(block, axes, distance):
    return lax.ppermute(block, ("layer", "feat"), route(axes, distance))


def ahead(block, pieces, axes):
    return [block] + [send(pieces[r], axes, -AWAY[r]) for r in (1, 2, 3)]


def behind(pieces, axes):
    return [pieces[0]] + [send(pieces[r], axes, AWAY[r]) for r in (1, 2, 3)]


def to_second(block):
    return lax.ppermute(block, "layer", [(0, 1)])


def to_first(block):
    return lax.ppermute(block, "layer", [(1, 0)])


def swapped(block):
    return lax.ppermute(block, "layer", [(0, 1), (1, 0)])


def line_gather(block, axes):
    return ahead(block, [block] * SIDE, axes)


def line_reduce(terms, axes):
    terms = behind([terms[0]] + [term.astype(BF16) for term in terms[1:]], axes)
    return sum(term.astype(F32) for term in terms)


def contract_rows(left, right):
    return lax.dot_general(left, right, (((0,), (0,)), ((), ())), preferred_element_type=F32)


def contract_cols(left, right):
    return lax.dot_general(left, right, (((1,), (1,)), ((), ())), preferred_element_type=F32)


def dot(left, right):
    return jnp.dot(left, right, preferred_element_type=F32)


def call(kernel, name, scalars, ins, outs, scratch=()):
    size = sum(a.size * a.dtype.itemsize for a in ins)
    vmem, smem = pl.BlockSpec(memory_space=pltpu.VMEM), pl.BlockSpec(memory_space=pltpu.SMEM)
    return pl.pallas_call(
        kernel,
        in_specs=[smem] + [vmem] * len(ins),
        out_specs=[pl.BlockSpec(memory_space=out[2]) if len(out) > 2 else vmem for out in outs],
        out_shape=[jax.ShapeDtypeStruct(out[0], out[1]) for out in outs],
        scratch_shapes=list(scratch),
        compiler_params=PARAMS,
        cost_estimate=pl.CostEstimate(flops=2**31, bytes_accessed=size, transcendentals=0),
        name=name,
    )(scalars, *ins)


class Writer:
    def __init__(self, sems):
        self.sems, self.started = sems, []

    def write(self, source, target):
        copy = pltpu.make_async_copy(source, target, self.sems.at[len(self.started)])
        copy.start()
        self.started.append(copy)

    def finish(self):
        for copy in self.started:
            copy.wait()


def sixths(width):
    step = width // 6
    return [pl.ds(j * step, step) for j in range(6)]


def stacked(pieces, cols):
    return jnp.concatenate([p[:, cols] for p in pieces], axis=0)


OWNER_AT, PLACE_AT, FLAG_AT = 16, 17, 18
TOO_MANY = -1e30


def select_kernel(s, *refs):
    pieces, outs = refs[:4], refs[4:8]
    pick_ref, spread_ref, flag_ref = refs[8:11]
    width = pieces[0].shape[1]
    tail = jnp.concatenate([p[:, width - BLK :] for p in pieces], axis=0).astype(F32)
    lane = lax.broadcasted_iota(jnp.int32, (PLANE, BLK), 1)
    row = lax.broadcasted_iota(jnp.int32, (PLANE, BLK), 0)
    numbers = jnp.where(lane < OWNER_AT, tail, 0.0)
    needs = jnp.zeros((PLANE, BLK), F32)
    for r in range(SIDE):
        low = (s[2 + r] * 4).astype(F32)
        inside = jnp.where((numbers > low + 0.5) & (numbers < low + 4.5), 1.0, 0.0)
        needs = jnp.where(lane == r, jnp.max(inside, axis=1, keepdims=True), needs)
    needs = needs.astype(BF16)
    upto = jnp.where(row <= lane, 1.0, 0.0).astype(BF16)
    same = jnp.where(row == lane, 1.0, 0.0).astype(BF16)
    down = jnp.where(lane <= row, 1.0, 0.0).astype(BF16)
    count_rows = contract_rows(needs, upto)
    need_rows = contract_rows(needs, same)
    count_cols = dot(down, needs)
    need_cols = needs.astype(F32)
    place = lax.broadcasted_iota(jnp.int32, (CAP, BLK), 0).astype(F32) + 1.0
    for r in range(SIDE):
        hit = (count_rows[r : r + 1, :] == place) & (need_rows[r : r + 1, :] > 0.5)
        pick_ref[pl.ds(r * CAP, CAP), :] = jnp.where(hit, 1.0, 0.0).astype(BF16)
    half = lane < CAP
    place = jnp.where(half, lane, lane - CAP).astype(F32) + 1.0
    for pair in range(2):
        a, b = 2 * pair, 2 * pair + 1
        count = jnp.where(half, count_cols[:, a : a + 1], count_cols[:, b : b + 1])
        need = jnp.where(half, need_cols[:, a : a + 1], need_cols[:, b : b + 1])
        hit = (count == place) & (need > 0.5)
        spread_ref[:, pl.ds(pair * BLK, BLK)] = jnp.where(hit, 1.0, 0.0).astype(BF16)
    most = jnp.max(jnp.max(count_cols, axis=1, keepdims=True), axis=0, keepdims=True)
    flag_ref[...] = jnp.broadcast_to(jnp.where(most > CAP + 0.5, 1.0, 0.0), flag_ref.shape).astype(BF16)
    pick = pick_ref[...]
    for at in range(0, width, 1024):
        cols = pl.ds(at, min(1024, width - at))
        plane = jnp.concatenate([p[:, cols] for p in pieces], axis=0)
        chosen = dot(pick, plane).astype(BF16)
        for r in range(SIDE):
            outs[r][:, cols] = chosen[r * CAP : (r + 1) * CAP]


def select(scalars, pieces):
    width = pieces[0].shape[1]
    outs = [((CAP, width), BF16)] * 4 + [((ROWS, PLANE), BF16), ((PLANE, ROWS), BF16), ((CAP, BLK), BF16)]
    *chosen, pick, spread, flag = call(select_kernel, "select", scalars, pieces, outs)
    return chosen, pick, spread, flag


def encode_kernel(slots, s, *refs):
    pieces, w_ref, b_ref, flag_ref = refs[:4], *refs[4:7]
    codes_ref, gate_ref, acc = refs[7:10]
    width, latents = w_ref.shape[1:]
    acc[...] = jnp.broadcast_to(b_ref[...], acc.shape)
    for cols in sixths(width):
        acc[...] += dot(stacked(pieces, cols), w_ref[0, cols, :])
    lane = lax.broadcasted_iota(jnp.int32, (CAP, BLK), 1)
    for r in range(SIDE):
        rows = pl.ds(r * CAP, CAP)
        tail = pieces[r][:, pl.ds(width, BLK)]
        codes_ref[rows, pl.ds(latents, BLK)] = jnp.where(lane == FLAG_AT, flag_ref[...].astype(F32), tail.astype(F32)).astype(BF16)
        here = jnp.where(lane < slots, tail.astype(F32), 0.0)
        for b in range(latents // BLK):
            number = (s[0] * (latents // BLK) + (b + 1)).astype(F32)
            active = jnp.max(jnp.where(here == number, 1.0, 0.0), axis=1, keepdims=True)
            pre = acc[rows, pl.ds(b * BLK, BLK)]
            decay = jnp.exp(-jnp.abs(pre))
            soft = jnp.maximum(pre, 0.0) + jnp.log1p(decay)
            slope = jnp.where(pre >= 0, 1.0, decay) / (1.0 + decay)
            codes_ref[rows, pl.ds(b * BLK, BLK)] = (active * soft).astype(BF16)
            gate_ref[rows, pl.ds(b * BLK, BLK)] = active * slope


def encode(scalars, pieces, w_enc, b_enc, flag, slots):
    latents = w_enc.shape[2]
    outs = [((ROWS, latents + BLK), BF16), ((ROWS, latents), F32)]
    kernel = functools.partial(encode_kernel, slots)
    return call(kernel, "encode", scalars, [*pieces, w_enc, b_enc, flag], outs, [pltpu.VMEM((ROWS, latents), F32)])


def decode_self_kernel(slots, s, codes_ref, w_ref, sum_ref, slot_ref):
    latents, width = w_ref.shape[1:]
    for cols in sixths(width):
        sum_ref[:, cols] = dot(codes_ref[:, pl.ds(0, latents)], w_ref[0, :, cols])
    lane = lax.broadcasted_iota(jnp.int32, (CAP, BLK), 1)
    for r in range(SIDE):
        rows = pl.ds(r * CAP, CAP)
        here = jnp.where(lane < slots, codes_ref[rows, pl.ds(latents, BLK)].astype(F32), 0.0)
        picked = [jnp.zeros((CAP, BLK), F32) for _ in range(slots)]
        for b in range(latents // BLK):
            number = (s[0] * (latents // BLK) + (b + 1)).astype(F32)
            wide = codes_ref[rows, pl.ds(b * BLK, BLK)].astype(F32)
            for k in range(slots):
                picked[k] = jnp.where(here[:, k : k + 1] == number, wide, picked[k])
        for k in range(slots):
            slot_ref[rows, pl.ds(k * BLK, BLK)] = picked[k].astype(BF16)


def decode_self(scalars, codes, w_self, slots):
    outs = [((ROWS, w_self.shape[2]), F32), ((ROWS, slots * BLK), BF16)]
    return call(functools.partial(decode_self_kernel, slots), "decode_self", scalars, [codes, w_self], outs)


def decode_kernel(s, own_ref, other_ref, sum_ref, cross_first_ref, cross_ref, slot_ref, *refs):
    outs, source_ref, match_ref = refs[:4], refs[4], refs[5]
    latents, half = cross_ref.shape
    width = 2 * half
    first = s[1] == 0
    own, other = own_ref[:, pl.ds(latents, BLK)], other_ref[:, pl.ds(latents, BLK)]
    one, zero = jnp.where(first, other, own), jnp.where(first, own, other)
    lane = lax.broadcasted_iota(jnp.int32, (8, BLK), 1)
    row = lax.broadcasted_iota(jnp.int32, (8, BLK), 0)
    take = jnp.where(lane == row + OWNER_AT, 1.0, 0.0).astype(BF16)

    def matched(cols, rows):
        numbers = contract_cols(take, rows)
        owner = cols[:, OWNER_AT : OWNER_AT + 1].astype(F32)
        place = cols[:, PLACE_AT : PLACE_AT + 1].astype(F32)
        hit = (owner == numbers[0:1]) & (place == numbers[1:2]) & (owner > 0.5)
        return jnp.where(hit, 1.0, 0.0).astype(BF16)

    match_ref[...] = matched(zero, one)
    codes = jnp.where(first, own_ref[:, pl.ds(0, latents)], other_ref[:, pl.ds(0, latents)])
    source_ref[...] = dot(matched(one, zero), codes).astype(BF16)
    slots = slot_ref.shape[1]
    flag = (own + other).astype(F32)[:CAP, FLAG_AT : FLAG_AT + 1]
    flag = jnp.broadcast_to(flag, (CAP, slots)) > 0.5
    for r in range(SIDE):
        slotted = jnp.where(flag, TOO_MANY, slot_ref[pl.ds(r * CAP, CAP), :].astype(F32))
        outs[r][:, pl.ds(width, slots)] = slotted.astype(BF16)

    def put(cols, value):
        value = value.astype(BF16)
        for r in range(SIDE):
            outs[r][:, cols] = value[r * CAP : (r + 1) * CAP]

    @pl.when(first)
    def _():
        for cols in sixths(width):
            put(cols, sum_ref[:, cols])

    @pl.when(jnp.logical_not(first))
    def _():
        for cols in sixths(width):
            cross = cross_first_ref[:, cols] if cols.start < half else cross_ref[:, pl.ds(cols.start - half, cols.size)]
            put(cols, sum_ref[:, cols] + dot(source_ref[...], cross))


def decode(scalars, own, other, self_sum, w_cross_first, w_cross, slotted):
    latents, half = w_cross.shape
    wide = 2 * half + slotted.shape[1]
    outs = [((CAP, wide), BF16)] * 4 + [((ROWS, latents), BF16), ((ROWS, ROWS), BF16)]
    ins = [own, other, self_sum, w_cross_first, w_cross, slotted]
    *sums, source, match = call(decode_kernel, "decode", scalars, ins, outs)
    return sums, source, match


def spread_kernel(main, s, spread_ref, *refs):
    pieces, outs = refs[:4], refs[4:]
    width = pieces[0].shape[1]
    step = 9 * BLK
    for at in range(0, width, step):
        cols = pl.ds(at, min(step, width - at))
        total = dot(spread_ref[...], stacked(pieces, cols)).astype(BF16)
        for m in range(SIDE):
            outs[m][:, cols] = total[m * LINE : (m + 1) * LINE]
    least = jnp.min(sum(p[0:16, pl.ds(main, BLK)].astype(F32) for p in pieces))

    @pl.when(least < -0.5)
    def _():
        for m in range(SIDE):
            outs[m][:, pl.ds(main, width - main)] = jnp.full((LINE, width - main), TOO_MANY, F32).astype(BF16)


def spread_sum(scalars, spread, pieces, main):
    outs = [((LINE, pieces[0].shape[1]), BF16)] * 4
    return call(functools.partial(spread_kernel, main), "spread", scalars, [spread, *pieces], outs)


def line_kernel(s, *refs):
    pieces, targets_ref, exact_ref, sents = refs[:4], refs[4], refs[5], refs[6:]
    tokens, width = targets_ref.shape[1:]
    for cols in sixths(width):
        total = sum(p[:, cols].astype(F32) for p in pieces)
        own = total[:tokens] - targets_ref[0, :, cols].astype(F32)
        total = jnp.concatenate([own, total[tokens:]], axis=0)
        exact_ref[:, cols] = total
        for sent in sents:
            sent[:, cols] = total.astype(BF16)
    slots = exact_ref.shape[1] - width
    quarter = slots // SIDE
    total = sum(p[:, pl.ds(width, slots)].astype(F32) for p in pieces)
    exact_ref[:, pl.ds(width, slots)] = total
    for r in (1, 2, 3):
        i = AWAY.index(-AWAY[r] % SIDE)
        rows = total[tokens * i : tokens * (i + 1)]
        folded = jnp.concatenate([rows[:, quarter * c : quarter * (c + 1)] for c in range(SIDE)], axis=0)
        sents[r - 1][:, pl.ds(width, quarter)] = folded.astype(BF16)


def line_terms(scalars, pieces, targets):
    rows, columns = pieces[0].shape
    width = targets.shape[2]
    outs = [((rows, columns), F32)] + [((rows, width + (columns - width) // SIDE), BF16)] * 3
    exact, *sents = call(line_kernel, "line", scalars, [*pieces, targets], outs)
    return exact, [exact, *sents]


def settle_kernel(s, exact_ref, *refs):
    came, err_ref, own_ref, tail_ref = refs[:3], *refs[3:]
    tokens, width = own_ref.shape
    for cols in sixths(width):
        total = exact_ref[:, cols]
        for r in (1, 2, 3):
            value = came[r - 1][:, cols].astype(F32)
            order = [AWAY.index((AWAY[j] - AWAY[r]) % SIDE) for j in range(SIDE)]
            total += jnp.concatenate([value[tokens * i : tokens * (i + 1)] for i in order], axis=0)
        err_ref[:, cols] = total.astype(BF16)
        own_ref[:, cols] = total[:tokens]
    slots = tail_ref.shape[1]
    tail = exact_ref[0:tokens, pl.ds(width, slots)]
    for r in (1, 2, 3):
        value = came[r - 1][:, pl.ds(width, slots // SIDE)].astype(F32)
        tail += jnp.concatenate([value[tokens * c : tokens * (c + 1)] for c in range(SIDE)], axis=1)
    tail_ref[...] = tail


def settle(scalars, exact, came, tokens, width):
    rows, columns = exact.shape
    outs = [((rows, width), BF16), ((tokens, width), F32), ((tokens, columns - width), F32)]
    return call(settle_kernel, "settle", scalars, [exact, *came], outs)


def compact_kernel(s, pick_ref, *refs):
    pieces, outs = refs[:4], refs[4:]
    for cols in sixths(pieces[0].shape[1]):
        chosen = dot(pick_ref[...], stacked(pieces, cols)).astype(BF16)
        for r in range(SIDE):
            outs[r][:, cols] = chosen[r * CAP : (r + 1) * CAP]


def compact(scalars, pick, pieces):
    outs = [((CAP, pieces[0].shape[1]), BF16)] * 4
    return call(compact_kernel, "compact", scalars, [pick, *pieces], outs)


def cross_kernel(s, match_ref, cross_first_ref, cross_ref, *refs):
    pieces, out_ref, acc = refs[:4], refs[4], refs[5]
    latents, half = cross_ref.shape

    @pl.when(s[1] != 0)
    def _():
        acc[...] = jnp.zeros(acc.shape, F32)
        for cols in sixths(2 * half):
            err = stacked(pieces, cols)
            if cols.start < half:
                out_ref[:, cols] = err
                acc[...] += contract_cols(err, cross_first_ref[:, cols])
            else:
                acc[...] += contract_cols(err, cross_ref[:, pl.ds(cols.start - half, cols.size)])
        value = acc[...]
        high = value.astype(BF16)
        rest = (value - high.astype(F32)).astype(BF16)
        turned = dot(match_ref[...], high) + dot(match_ref[...], rest)
        high = turned.astype(BF16)
        out_ref[:, pl.ds(half, latents)] = high
        out_ref[:, pl.ds(half + latents, latents)] = (turned - high.astype(F32)).astype(BF16)


def cross_back(scalars, match, pieces, w_cross_first, w_cross):
    latents, half = w_cross.shape
    outs = [((ROWS, half + 2 * latents), BF16)]
    ins = [match, w_cross_first, w_cross, *pieces]
    return call(cross_kernel, "cross_back", scalars, ins, outs, [pltpu.VMEM((ROWS, latents), F32)])[0]


def self_kernel(s, codes_ref, w_ref, *refs):
    pieces, term_ref, grad_ref, turned, grad, sems = refs[:4], *refs[4:]
    latents, width = w_ref.shape[1:]
    writer = Writer(sems)
    turned[...] = codes_ref[:, pl.ds(0, latents)].T
    term_ref[...] = jnp.zeros(term_ref.shape, F32)
    for cols in sixths(width):
        err = stacked(pieces, cols)
        grad[:, cols] = dot(turned[...], err).astype(BF16)
        writer.write(grad.at[:, cols], grad_ref.at[0, :, cols])
        term_ref[...] += contract_cols(err, w_ref[0, :, cols])
    writer.finish()


def self_back(scalars, codes, pieces, w_self):
    latents, width = w_self.shape[1:]
    outs = [((ROWS, latents), F32), (w_self.shape, BF16, pltpu.HBM)]
    scratch = [pltpu.VMEM((latents, ROWS), BF16), pltpu.VMEM((latents, width), BF16), pltpu.SemaphoreType.DMA((6,))]
    return call(self_kernel, "self_back", scalars, [codes, w_self, *pieces], outs, scratch)


def last_kernel(s, term_ref, gate_ref, source_ref, returned_ref, tail_ref, own_ref, targets_ref, *refs):
    x, errs = refs[:4], refs[4:8]
    enc_ref, bias_ref, cross_ref, picked_ref, recon_ref, again_ref = refs[8:14]
    dpre, turned, enc, cross, bias, picked, recon, sems = refs[14:]
    width, half = enc.shape[0], cross.shape[1]
    writer = Writer(sems)
    latents = dpre.shape[1]
    again_ref[0] = jnp.where(jnp.min(tail_ref[...]) < -0.5, 1, 0)
    back = [returned_ref[:, pl.ds(at, latents)].astype(F32) for at in (half, half + latents)]
    value = ((term_ref[...] + (back[0] + back[1])) * gate_ref[...]).astype(BF16)
    dpre[...] = value
    bias[...] = jnp.sum(value.astype(F32), axis=0, keepdims=True)
    writer.write(bias, bias_ref)
    recon[...] = own_ref[...] + targets_ref[0].astype(F32)
    writer.write(recon, recon_ref.at[0])
    tokens, slots = tail_ref.shape[0], tail_ref.shape[1] // BLK
    rows = [tail_ref[t : t + 1, pl.ds(k * BLK, BLK)] for t in range(tokens) for k in range(slots)]
    picked[...] = jnp.concatenate(rows, axis=0).astype(BF16)
    writer.write(picked, picked_ref)
    for cols in sixths(width):
        enc[cols, :] = contract_rows(stacked(x, cols), dpre[...]).astype(BF16)
        writer.write(enc.at[cols, :], enc_ref.at[0, cols, :])
    turned[...] = source_ref[...].T
    step = half // 3
    for j in range(3):
        cols = pl.ds(j * step, step)

        @pl.when(s[1] == 0)
        def _():
            cross[:, cols] = dot(turned[...], returned_ref[:, cols]).astype(BF16)

        @pl.when(s[1] != 0)
        def _():
            err = stacked(errs, pl.ds(half + cols.start, step))
            cross[:, cols] = dot(turned[...], err).astype(BF16)

        writer.write(cross.at[:, cols], cross_ref.at[:, cols])
    writer.finish()


def last(scalars, term, gate, source, returned, tail, own_err, targets, x, errs):
    latents, half = source.shape[1], returned.shape[1] - 2 * source.shape[1]
    picked = ((tail.shape[0] * tail.shape[1] // BLK, BLK), BF16)
    enc, bias, cross = ((2 * half, latents), BF16), ((1, latents), F32), ((latents, half), BF16)
    recon = (own_err.shape, F32)
    outs = [((1, *enc[0]), BF16), bias, cross, picked, ((1, *recon[0]), F32)]
    outs = [(*out, pltpu.HBM) for out in outs] + [((1,), jnp.int32, pltpu.SMEM)]
    scratch = [((ROWS, latents), BF16), ((latents, ROWS), BF16), enc, cross, bias, picked, recon]
    scratch = [pltpu.VMEM(*what) for what in scratch] + [pltpu.SemaphoreType.DMA((12,))]
    ins = [term, gate, source, returned, tail, own_err, targets, *x, *errs]
    return call(last_kernel, "last", scalars, ins, outs, scratch)


def reorder(rows, axes):
    shape = (SIDE, SIDE, SIDE, -1, rows.shape[-1])
    return jnp.transpose(rows.reshape(shape), (*axes, 3, 4)).reshape(rows.shape)


def to_second_order(rows):
    return reorder(rows, (2, 0, 1))


def to_first_order(rows):
    return reorder(rows, (1, 2, 0))


def gather_all(rows):
    for axes in (INNER, MIDDLE, OUTER):
        rows = jnp.concatenate(line_gather(rows, axes), axis=0)
    return rows


def reduce_all(rows):
    for axes in (OUTER, MIDDLE, INNER):
        rows = line_reduce(jnp.split(rows, SIDE, axis=0), axes)
    return rows


def dense(inputs, targets, w_enc, b_enc, w_self, w_cross, block_ids, w_cross_first):
    first_layer = lax.axis_index("layer") == 0
    width = inputs.shape[2]
    half = width // 2
    blocks = w_enc.shape[2] // BLK
    slots = block_ids.shape[2]
    tail = jnp.pad(block_ids[0].astype(BF16), ((0, 0), (0, BLK - slots)))
    gathered = gather_all(jnp.concatenate([inputs[0], tail], axis=1))
    x, ids = gathered[:, :width], gathered[:, width : width + slots].astype(jnp.int32)
    own_blocks = lax.axis_index("feat") * blocks + jnp.arange(blocks, dtype=jnp.int32)
    hit = ids[:, :, None] == own_blocks[None, None, :]
    active = jnp.repeat(jnp.any(hit, axis=1), BLK, axis=1).astype(F32)
    pre = dot(x, w_enc[0]) + b_enc[0]
    codes = (active * jax.nn.softplus(pre)).astype(BF16)
    turned = to_second_order(codes)
    earlier = to_second(turned)
    source = jnp.where(first_layer, turned, earlier)
    by_block = codes.reshape(-1, 1, blocks, BLK)
    slotted = jnp.sum(jnp.where(hit[..., None], by_block, 0).astype(F32), axis=2).reshape(-1, slots * BLK)
    w_cross_all = jnp.concatenate([w_cross_first, w_cross], axis=1)
    partial = dot(codes, w_self[0]) + dot(earlier, w_cross_all)
    summed = reduce_all(jnp.concatenate([partial, slotted], axis=1).astype(BF16))
    recon = summed[:, :width]
    picked = summed[:, width:].astype(BF16).reshape(-1, slots, BLK)
    err = gather_all((recon - targets[0].astype(F32)).astype(BF16))
    back = to_first_order(to_first(contract_cols(err, w_cross_all)))
    returned = to_first(err[:, :half])
    term = contract_cols(err, w_self[0])
    grad_self = contract_rows(codes, err).astype(BF16)
    cross_err = jnp.where(first_layer, returned, err[:, half:])
    grad_cross = contract_rows(source, cross_err).astype(BF16)
    code_grads = term + jnp.where(first_layer, back, 0.0)
    pre_grads = (code_grads * active * jax.nn.sigmoid(pre)).astype(BF16)
    grad_enc = contract_rows(x, pre_grads).astype(BF16)
    grad_benc = jnp.sum(pre_grads.astype(F32), axis=0)
    return recon, picked, grad_enc, grad_benc[None], grad_self, grad_cross


def per_device(inputs, targets, w_enc, b_enc, w_self, w_cross, block_ids):
    layer = lax.axis_index("layer")
    shard = lax.axis_index("feat")
    width = inputs.shape[2]
    slots = block_ids.shape[2]
    tokens_dev = inputs.shape[1]

    y, z = shard // (SIDE * SIDE), shard % SIDE
    receivers = [
        jnp.where(layer == 0, shard - z + (z - r) % SIDE, shard + SIDE * SIDE * ((y - r) % SIDE - y))
        for r in AWAY
    ]
    scalars = jnp.stack([shard, layer] + receivers).astype(jnp.int32)

    own_ids, other_ids = (ids[0].astype(BF16) + 1 for ids in (block_ids, swapped(block_ids)))
    owner = jnp.full((tokens_dev, 1), shard + 1).astype(BF16)
    place = jnp.arange(tokens_dev, dtype=jnp.int32)[:, None].astype(BF16)
    spare = jnp.zeros((tokens_dev, BLK - 2 * slots - 2), BF16)
    rows = jnp.concatenate([inputs[0], own_ids, other_ids, owner, place, spare], axis=1)

    line = jnp.concatenate(line_gather(rows, INNER), axis=0)
    chosen, pick, spread, flag = select(scalars, line_gather(line, MIDDLE))
    x = ahead(chosen[0], chosen, OUTER)
    x, half_cross = lax.optimization_barrier((x, w_cross))
    w_cross_first = to_second(half_cross)
    codes, gate = encode(scalars, x, w_enc, b_enc, flag, slots)
    other_codes = swapped(codes)
    self_sum, slotted = decode_self(scalars, codes, w_self, slots)
    sums, source, match = decode(scalars, codes, other_codes, self_sum, w_cross_first, w_cross, slotted)
    sums = behind(sums, OUTER)
    exact, sents = line_terms(scalars, behind(spread_sum(scalars, spread, sums, width), MIDDLE), targets)
    err_line, own_err, tail = settle(scalars, exact, ahead(exact, sents, INNER)[1:], tokens_dev, width)
    err_plane = line_gather(err_line, MIDDLE)
    kept = compact(scalars, pick, err_plane)
    errs = ahead(kept[0], kept, OUTER)
    returned = to_first(cross_back(scalars, match, errs, w_cross_first, w_cross))
    term, grad_self = self_back(scalars, codes, errs, w_self)
    grad_enc, grad_benc, grad_cross, picked, recon, again = last(
        scalars, term, gate, source, returned, tail, own_err, targets, x, errs
    )

    def on_every_row(_):
        results = dense(inputs, targets, w_enc, b_enc, w_self, w_cross, block_ids, w_cross_first)
        recon, picked, grad_enc, grad_benc, grad_self, grad_cross = results
        return jnp.int32(0), recon[None], picked.reshape(-1, BLK), grad_enc[None], grad_benc, grad_self[None], grad_cross

    results = (again[0], recon, picked, grad_enc, grad_benc, grad_self, grad_cross)
    _, recon, picked, *grads = lax.while_loop(lambda carried: carried[0] > 0, on_every_row, results)
    return recon, picked.reshape(1, tokens_dev, slots, BLK), *grads


def solution(mesh):
    placed = (
        P("layer", "feat", None),
        P("layer", "feat", None),
        P("layer", None, "feat"),
        P("layer", "feat"),
        P("layer", "feat", None),
        P("feat", "layer"),
        P("layer", "feat", None),
    )
    return jax.shard_map(
        per_device,
        mesh=mesh,
        in_specs=placed,
        out_specs=(
            P("layer", "feat", None),
            P("layer", "feat", None, None),
            P("layer", None, "feat"),
            P("layer", "feat"),
            P("layer", "feat", None),
            P("feat", "layer"),
        ),
        check_vma=False,
    )
```

```python
import functools

import jax
import jax.numpy as jnp
from jax import lax
from jax.experimental import pallas as pl
from jax.experimental.pallas import tpu as pltpu
from jax.sharding import PartitionSpec as P

BLK = 128
SIDE = 4
LINE = 32
PLANE = 128
CAP = 64
ROWS = SIDE * CAP
AWAY = (0, 2, 3, 1)
STEPS = {"y": (1, 0, 0), "x": (0, 1, 0), "z": (0, 0, 1)}
F32, BF16 = jnp.float32, jnp.bfloat16

OUTER = ("z", "y")
MIDDLE = ("x", "z")
INNER = ("y", "x")

PARAMS = pltpu.CompilerParams(vmem_limit_bytes=20 * 2**20)


def route(axes, distance):
    pairs = []
    for core, axis in enumerate(axes):
        step = STEPS[axis]
        for y in range(SIDE):
            for x in range(SIDE):
                for z in range(SIDE):
                    there = [(c + distance * s) % SIDE for c, s in zip((y, x, z), step)]
                    base = core * SIDE**3
                    pairs.append(
                        (base + (y * SIDE + x) * SIDE + z, base + (there[0] * SIDE + there[1]) * SIDE + there[2])
                    )
    return pairs


def send(block, axes, distance):
    return lax.ppermute(block, ("layer", "feat"), route(axes, distance))


def ahead(block, pieces, axes):
    return [block] + [send(pieces[r], axes, -AWAY[r]) for r in (1, 2, 3)]


def behind(pieces, axes):
    return [pieces[0]] + [send(pieces[r], axes, AWAY[r]) for r in (1, 2, 3)]


def to_second(block):
    return lax.ppermute(block, "layer", [(0, 1)])


def to_first(block):
    return lax.ppermute(block, "layer", [(1, 0)])


def swapped(block):
    return lax.ppermute(block, "layer", [(0, 1), (1, 0)])


def line_gather(block, axes):
    return ahead(block, [block] * SIDE, axes)


def line_reduce(terms, axes):
    terms = behind([terms[0]] + [term.astype(BF16) for term in terms[1:]], axes)
    return sum(term.astype(F32) for term in terms)


def contract_rows(left, right):
    return lax.dot_general(left, right, (((0,), (0,)), ((), ())), preferred_element_type=F32)


def contract_cols(left, right):
    return lax.dot_general(left, right, (((1,), (1,)), ((), ())), preferred_element_type=F32)


def dot(left, right):
    return jnp.dot(left, right, preferred_element_type=F32)


def call(kernel, name, scalars, ins, outs, scratch=()):
    size = sum(a.size * a.dtype.itemsize for a in ins)
    vmem, smem = pl.BlockSpec(memory_space=pltpu.VMEM), pl.BlockSpec(memory_space=pltpu.SMEM)
    return pl.pallas_call(
        kernel,
        in_specs=[smem] + [vmem] * len(ins),
        out_specs=[pl.BlockSpec(memory_space=out[2]) if len(out) > 2 else vmem for out in outs],
        out_shape=[jax.ShapeDtypeStruct(out[0], out[1]) for out in outs],
        scratch_shapes=list(scratch),
        compiler_params=PARAMS,
        cost_estimate=pl.CostEstimate(flops=2**31, bytes_accessed=size, transcendentals=0),
        name=name,
    )(scalars, *ins)


class Writer:
    def __init__(self, sems):
        self.sems, self.started = sems, []

    def write(self, source, target):
        copy = pltpu.make_async_copy(source, target, self.sems.at[len(self.started)])
        copy.start()
        self.started.append(copy)

    def finish(self):
        for copy in self.started:
            copy.wait()


def sixths(width):
    step = width // 6
    return [pl.ds(j * step, step) for j in range(6)]


def stacked(pieces, cols):
    return jnp.concatenate([p[:, cols] for p in pieces], axis=0)


OWNER_AT, PLACE_AT, FLAG_AT = 16, 17, 18
TOO_MANY = -1e30


def select_kernel(s, *refs):
    pieces, outs = refs[:4], refs[4:8]
    pick_ref, spread_ref, flag_ref = refs[8:11]
    width = pieces[0].shape[1]
    tail = jnp.concatenate([p[:, width - BLK :] for p in pieces], axis=0).astype(F32)
    lane = lax.broadcasted_iota(jnp.int32, (PLANE, BLK), 1)
    row = lax.broadcasted_iota(jnp.int32, (PLANE, BLK), 0)
    numbers = jnp.where(lane < OWNER_AT, tail, 0.0)
    needs = jnp.zeros((PLANE, BLK), F32)
    for r in range(SIDE):
        low = (s[2 + r] * 4).astype(F32)
        inside = jnp.where((numbers > low + 0.5) & (numbers < low + 4.5), 1.0, 0.0)
        needs = jnp.where(lane == r, jnp.max(inside, axis=1, keepdims=True), needs)
    needs = needs.astype(BF16)
    upto = jnp.where(row <= lane, 1.0, 0.0).astype(BF16)
    same = jnp.where(row == lane, 1.0, 0.0).astype(BF16)
    down = jnp.where(lane <= row, 1.0, 0.0).astype(BF16)
    count_rows = contract_rows(needs, upto)
    need_rows = contract_rows(needs, same)
    count_cols = dot(down, needs)
    need_cols = needs.astype(F32)
    place = lax.broadcasted_iota(jnp.int32, (CAP, BLK), 0).astype(F32) + 1.0
    for r in range(SIDE):
        hit = (count_rows[r : r + 1, :] == place) & (need_rows[r : r + 1, :] > 0.5)
        pick_ref[pl.ds(r * CAP, CAP), :] = jnp.where(hit, 1.0, 0.0).astype(BF16)
    half = lane < CAP
    place = jnp.where(half, lane, lane - CAP).astype(F32) + 1.0
    for pair in range(2):
        a, b = 2 * pair, 2 * pair + 1
        count = jnp.where(half, count_cols[:, a : a + 1], count_cols[:, b : b + 1])
        need = jnp.where(half, need_cols[:, a : a + 1], need_cols[:, b : b + 1])
        hit = (count == place) & (need > 0.5)
        spread_ref[:, pl.ds(pair * BLK, BLK)] = jnp.where(hit, 1.0, 0.0).astype(BF16)
    most = jnp.max(jnp.max(count_cols, axis=1, keepdims=True), axis=0, keepdims=True)
    flag_ref[...] = jnp.broadcast_to(jnp.where(most > CAP + 0.5, 1.0, 0.0), flag_ref.shape).astype(BF16)
    pick = pick_ref[...]
    for at in range(0, width, 1024):
        cols = pl.ds(at, min(1024, width - at))
        plane = jnp.concatenate([p[:, cols] for p in pieces], axis=0)
        chosen = dot(pick, plane).astype(BF16)
        for r in range(SIDE):
            outs[r][:, cols] = chosen[r * CAP : (r + 1) * CAP]


def select(scalars, pieces):
    width = pieces[0].shape[1]
    outs = [((CAP, width), BF16)] * 4 + [((ROWS, PLANE), BF16), ((PLANE, ROWS), BF16), ((CAP, BLK), BF16)]
    *chosen, pick, spread, flag = call(select_kernel, "select", scalars, pieces, outs)
    return chosen, pick, spread, flag


def encode_kernel(slots, s, *refs):
    pieces, w_ref, b_ref, flag_ref = refs[:4], *refs[4:7]
    codes_ref, gate_ref, acc = refs[7:10]
    width, latents = w_ref.shape[1:]
    acc[...] = jnp.broadcast_to(b_ref[...], acc.shape)
    for cols in sixths(width):
        acc[...] += dot(stacked(pieces, cols), w_ref[0, cols, :])
    lane = lax.broadcasted_iota(jnp.int32, (CAP, BLK), 1)
    for r in range(SIDE):
        rows = pl.ds(r * CAP, CAP)
        tail = pieces[r][:, pl.ds(width, BLK)]
        codes_ref[rows, pl.ds(latents, BLK)] = jnp.where(lane == FLAG_AT, flag_ref[...].astype(F32), tail.astype(F32)).astype(BF16)
        here = jnp.where(lane < slots, tail.astype(F32), 0.0)
        for b in range(latents // BLK):
            number = (s[0] * (latents // BLK) + (b + 1)).astype(F32)
            active = jnp.max(jnp.where(here == number, 1.0, 0.0), axis=1, keepdims=True)
            pre = acc[rows, pl.ds(b * BLK, BLK)]
            decay = jnp.exp(-jnp.abs(pre))
            soft = jnp.maximum(pre, 0.0) + jnp.log1p(decay)
            slope = jnp.where(pre >= 0, 1.0, decay) / (1.0 + decay)
            codes_ref[rows, pl.ds(b * BLK, BLK)] = (active * soft).astype(BF16)
            gate_ref[rows, pl.ds(b * BLK, BLK)] = active * slope


def encode(scalars, pieces, w_enc, b_enc, flag, slots):
    latents = w_enc.shape[2]
    outs = [((ROWS, latents + BLK), BF16), ((ROWS, latents), F32)]
    kernel = functools.partial(encode_kernel, slots)
    return call(kernel, "encode", scalars, [*pieces, w_enc, b_enc, flag], outs, [pltpu.VMEM((ROWS, latents), F32)])


def decode_self_kernel(slots, s, codes_ref, w_ref, sum_ref, slot_ref):
    latents, width = w_ref.shape[1:]
    for cols in sixths(width):
        sum_ref[:, cols] = dot(codes_ref[:, pl.ds(0, latents)], w_ref[0, :, cols])
    lane = lax.broadcasted_iota(jnp.int32, (CAP, BLK), 1)
    for r in range(SIDE):
        rows = pl.ds(r * CAP, CAP)
        here = jnp.where(lane < slots, codes_ref[rows, pl.ds(latents, BLK)].astype(F32), 0.0)
        picked = [jnp.zeros((CAP, BLK), F32) for _ in range(slots)]
        for b in range(latents // BLK):
            number = (s[0] * (latents // BLK) + (b + 1)).astype(F32)
            wide = codes_ref[rows, pl.ds(b * BLK, BLK)].astype(F32)
            for k in range(slots):
                picked[k] = jnp.where(here[:, k : k + 1] == number, wide, picked[k])
        for k in range(slots):
            slot_ref[rows, pl.ds(k * BLK, BLK)] = picked[k].astype(BF16)


def decode_self(scalars, codes, w_self, slots):
    outs = [((ROWS, w_self.shape[2]), F32), ((ROWS, slots * BLK), BF16)]
    return call(functools.partial(decode_self_kernel, slots), "decode_self", scalars, [codes, w_self], outs)


def decode_kernel(s, own_ref, other_ref, sum_ref, cross_first_ref, cross_ref, slot_ref, *refs):
    outs, source_ref, match_ref = refs[:4], refs[4], refs[5]
    latents, half = cross_ref.shape
    width = 2 * half
    first = s[1] == 0
    own, other = own_ref[:, pl.ds(latents, BLK)], other_ref[:, pl.ds(latents, BLK)]
    one, zero = jnp.where(first, other, own), jnp.where(first, own, other)
    lane = lax.broadcasted_iota(jnp.int32, (8, BLK), 1)
    row = lax.broadcasted_iota(jnp.int32, (8, BLK), 0)
    take = jnp.where(lane == row + OWNER_AT, 1.0, 0.0).astype(BF16)

    def matched(cols, rows):
        numbers = contract_cols(take, rows)
        owner = cols[:, OWNER_AT : OWNER_AT + 1].astype(F32)
        place = cols[:, PLACE_AT : PLACE_AT + 1].astype(F32)
        hit = (owner == numbers[0:1]) & (place == numbers[1:2]) & (owner > 0.5)
        return jnp.where(hit, 1.0, 0.0).astype(BF16)

    match_ref[...] = matched(zero, one)
    codes = jnp.where(first, own_ref[:, pl.ds(0, latents)], other_ref[:, pl.ds(0, latents)])
    source_ref[...] = dot(matched(one, zero), codes).astype(BF16)
    slots = slot_ref.shape[1]
    flag = (own + other).astype(F32)[:CAP, FLAG_AT : FLAG_AT + 1]
    flag = jnp.broadcast_to(flag, (CAP, slots)) > 0.5
    for r in range(SIDE):
        slotted = jnp.where(flag, TOO_MANY, slot_ref[pl.ds(r * CAP, CAP), :].astype(F32))
        outs[r][:, pl.ds(width, slots)] = slotted.astype(BF16)

    def put(cols, value):
        value = value.astype(BF16)
        for r in range(SIDE):
            outs[r][:, cols] = value[r * CAP : (r + 1) * CAP]

    @pl.when(first)
    def _():
        for cols in sixths(width):
            put(cols, sum_ref[:, cols])

    @pl.when(jnp.logical_not(first))
    def _():
        for cols in sixths(width):
            cross = cross_first_ref[:, cols] if cols.start < half else cross_ref[:, pl.ds(cols.start - half, cols.size)]
            put(cols, sum_ref[:, cols] + dot(source_ref[...], cross))


def decode(scalars, own, other, self_sum, w_cross_first, w_cross, slotted):
    latents, half = w_cross.shape
    wide = 2 * half + slotted.shape[1]
    outs = [((CAP, wide), BF16)] * 4 + [((ROWS, latents), BF16), ((ROWS, ROWS), BF16)]
    ins = [own, other, self_sum, w_cross_first, w_cross, slotted]
    *sums, source, match = call(decode_kernel, "decode", scalars, ins, outs)
    return sums, source, match


def spread_kernel(main, s, spread_ref, *refs):
    pieces, outs = refs[:4], refs[4:]
    width = pieces[0].shape[1]
    step = 9 * BLK
    for at in range(0, width, step):
        cols = pl.ds(at, min(step, width - at))
        total = dot(spread_ref[...], stacked(pieces, cols)).astype(BF16)
        for m in range(SIDE):
            outs[m][:, cols] = total[m * LINE : (m + 1) * LINE]
    least = jnp.min(sum(p[0:16, pl.ds(main, BLK)].astype(F32) for p in pieces))

    @pl.when(least < -0.5)
    def _():
        for m in range(SIDE):
            outs[m][:, pl.ds(main, width - main)] = jnp.full((LINE, width - main), TOO_MANY, F32).astype(BF16)


def spread_sum(scalars, spread, pieces, main):
    outs = [((LINE, pieces[0].shape[1]), BF16)] * 4
    return call(functools.partial(spread_kernel, main), "spread", scalars, [spread, *pieces], outs)


def line_kernel(s, *refs):
    pieces, targets_ref, exact_ref, sents = refs[:4], refs[4], refs[5], refs[6:]
    tokens, width = targets_ref.shape[1:]
    for cols in sixths(width):
        total = sum(p[:, cols].astype(F32) for p in pieces)
        own = total[:tokens] - targets_ref[0, :, cols].astype(F32)
        total = jnp.concatenate([own, total[tokens:]], axis=0)
        exact_ref[:, cols] = total
        for sent in sents:
            sent[:, cols] = total.astype(BF16)
    slots = exact_ref.shape[1] - width
    quarter = slots // SIDE
    total = sum(p[:, pl.ds(width, slots)].astype(F32) for p in pieces)
    exact_ref[:, pl.ds(width, slots)] = total
    for r in (1, 2, 3):
        i = AWAY.index(-AWAY[r] % SIDE)
        rows = total[tokens * i : tokens * (i + 1)]
        folded = jnp.concatenate([rows[:, quarter * c : quarter * (c + 1)] for c in range(SIDE)], axis=0)
        sents[r - 1][:, pl.ds(width, quarter)] = folded.astype(BF16)


def line_terms(scalars, pieces, targets):
    rows, columns = pieces[0].shape
    width = targets.shape[2]
    outs = [((rows, columns), F32)] + [((rows, width + (columns - width) // SIDE), BF16)] * 3
    exact, *sents = call(line_kernel, "line", scalars, [*pieces, targets], outs)
    return exact, [exact, *sents]


def settle_kernel(s, exact_ref, *refs):
    came, err_ref, own_ref, tail_ref = refs[:3], *refs[3:]
    tokens, width = own_ref.shape
    for cols in sixths(width):
        total = exact_ref[:, cols]
        for r in (1, 2, 3):
            value = came[r - 1][:, cols].astype(F32)
            order = [AWAY.index((AWAY[j] - AWAY[r]) % SIDE) for j in range(SIDE)]
            total += jnp.concatenate([value[tokens * i : tokens * (i + 1)] for i in order], axis=0)
        err_ref[:, cols] = total.astype(BF16)
        own_ref[:, cols] = total[:tokens]
    slots = tail_ref.shape[1]
    tail = exact_ref[0:tokens, pl.ds(width, slots)]
    for r in (1, 2, 3):
        value = came[r - 1][:, pl.ds(width, slots // SIDE)].astype(F32)
        tail += jnp.concatenate([value[tokens * c : tokens * (c + 1)] for c in range(SIDE)], axis=1)
    tail_ref[...] = tail


def settle(scalars, exact, came, tokens, width):
    rows, columns = exact.shape
    outs = [((rows, width), BF16), ((tokens, width), F32), ((tokens, columns - width), F32)]
    return call(settle_kernel, "settle", scalars, [exact, *came], outs)


def compact_kernel(s, pick_ref, *refs):
    pieces, outs = refs[:4], refs[4:]
    for cols in sixths(pieces[0].shape[1]):
        chosen = dot(pick_ref[...], stacked(pieces, cols)).astype(BF16)
        for r in range(SIDE):
            outs[r][:, cols] = chosen[r * CAP : (r + 1) * CAP]


def compact(scalars, pick, pieces):
    outs = [((CAP, pieces[0].shape[1]), BF16)] * 4
    return call(compact_kernel, "compact", scalars, [pick, *pieces], outs)


def cross_kernel(s, match_ref, cross_first_ref, cross_ref, *refs):
    pieces, out_ref, acc = refs[:4], refs[4], refs[5]
    latents, half = cross_ref.shape

    @pl.when(s[1] != 0)
    def _():
        acc[...] = jnp.zeros(acc.shape, F32)
        for cols in sixths(2 * half):
            err = stacked(pieces, cols)
            if cols.start < half:
                out_ref[:, cols] = err
                acc[...] += contract_cols(err, cross_first_ref[:, cols])
            else:
                acc[...] += contract_cols(err, cross_ref[:, pl.ds(cols.start - half, cols.size)])
        value = acc[...]
        high = value.astype(BF16)
        rest = (value - high.astype(F32)).astype(BF16)
        turned = dot(match_ref[...], high) + dot(match_ref[...], rest)
        high = turned.astype(BF16)
        out_ref[:, pl.ds(half, latents)] = high
        out_ref[:, pl.ds(half + latents, latents)] = (turned - high.astype(F32)).astype(BF16)


def cross_back(scalars, match, pieces, w_cross_first, w_cross):
    latents, half = w_cross.shape
    outs = [((ROWS, half + 2 * latents), BF16)]
    ins = [match, w_cross_first, w_cross, *pieces]
    return call(cross_kernel, "cross_back", scalars, ins, outs, [pltpu.VMEM((ROWS, latents), F32)])[0]


def self_kernel(s, codes_ref, w_ref, *refs):
    pieces, term_ref, grad_ref, turned, grad, sems = refs[:4], *refs[4:]
    latents, width = w_ref.shape[1:]
    writer = Writer(sems)
    turned[...] = codes_ref[:, pl.ds(0, latents)].T
    term_ref[...] = jnp.zeros(term_ref.shape, F32)
    for cols in sixths(width):
        err = stacked(pieces, cols)
        grad[:, cols] = dot(turned[...], err).astype(BF16)
        writer.write(grad.at[:, cols], grad_ref.at[0, :, cols])
        term_ref[...] += contract_cols(err, w_ref[0, :, cols])
    writer.finish()


def self_back(scalars, codes, pieces, w_self):
    latents, width = w_self.shape[1:]
    outs = [((ROWS, latents), F32), (w_self.shape, BF16, pltpu.HBM)]
    scratch = [pltpu.VMEM((latents, ROWS), BF16), pltpu.VMEM((latents, width), BF16), pltpu.SemaphoreType.DMA((6,))]
    return call(self_kernel, "self_back", scalars, [codes, w_self, *pieces], outs, scratch)


def last_kernel(s, term_ref, gate_ref, source_ref, returned_ref, tail_ref, own_ref, targets_ref, *refs):
    x, errs = refs[:4], refs[4:8]
    enc_ref, bias_ref, cross_ref, picked_ref, recon_ref, again_ref = refs[8:14]
    dpre, turned, enc, cross, bias, picked, recon, sems = refs[14:]
    width, half = enc.shape[0], cross.shape[1]
    writer = Writer(sems)
    latents = dpre.shape[1]
    again_ref[0] = jnp.where(jnp.min(tail_ref[...]) < -0.5, 1, 0)
    back = [returned_ref[:, pl.ds(at, latents)].astype(F32) for at in (half, half + latents)]
    value = ((term_ref[...] + (back[0] + back[1])) * gate_ref[...]).astype(BF16)
    dpre[...] = value
    bias[...] = jnp.sum(value.astype(F32), axis=0, keepdims=True)
    writer.write(bias, bias_ref)
    recon[...] = own_ref[...] + targets_ref[0].astype(F32)
    writer.write(recon, recon_ref.at[0])
    tokens, slots = tail_ref.shape[0], tail_ref.shape[1] // BLK
    rows = [tail_ref[t : t + 1, pl.ds(k * BLK, BLK)] for t in range(tokens) for k in range(slots)]
    picked[...] = jnp.concatenate(rows, axis=0).astype(BF16)
    writer.write(picked, picked_ref)
    for cols in sixths(width):
        enc[cols, :] = contract_rows(stacked(x, cols), dpre[...]).astype(BF16)
        writer.write(enc.at[cols, :], enc_ref.at[0, cols, :])
    turned[...] = source_ref[...].T
    step = half // 3
    for j in range(3):
        cols = pl.ds(j * step, step)

        @pl.when(s[1] == 0)
        def _():
            cross[:, cols] = dot(turned[...], returned_ref[:, cols]).astype(BF16)

        @pl.when(s[1] != 0)
        def _():
            err = stacked(errs, pl.ds(half + cols.start, step))
            cross[:, cols] = dot(turned[...], err).astype(BF16)

        writer.write(cross.at[:, cols], cross_ref.at[:, cols])
    writer.finish()


def last(scalars, term, gate, source, returned, tail, own_err, targets, x, errs):
    latents, half = source.shape[1], returned.shape[1] - 2 * source.shape[1]
    picked = ((tail.shape[0] * tail.shape[1] // BLK, BLK), BF16)
    enc, bias, cross = ((2 * half, latents), BF16), ((1, latents), F32), ((latents, half), BF16)
    recon = (own_err.shape, F32)
    outs = [((1, *enc[0]), BF16), bias, cross, picked, ((1, *recon[0]), F32)]
    outs = [(*out, pltpu.HBM) for out in outs] + [((1,), jnp.int32, pltpu.SMEM)]
    scratch = [((ROWS, latents), BF16), ((latents, ROWS), BF16), enc, cross, bias, picked, recon]
    scratch = [pltpu.VMEM(*what) for what in scratch] + [pltpu.SemaphoreType.DMA((12,))]
    ins = [term, gate, source, returned, tail, own_err, targets, *x, *errs]
    return call(last_kernel, "last", scalars, ins, outs, scratch)


def reorder(rows, axes):
    shape = (SIDE, SIDE, SIDE, -1, rows.shape[-1])
    return jnp.transpose(rows.reshape(shape), (*axes, 3, 4)).reshape(rows.shape)


def to_second_order(rows):
    return reorder(rows, (2, 0, 1))


def to_first_order(rows):
    return reorder(rows, (1, 2, 0))


def gather_all(rows):
    for axes in (INNER, MIDDLE, OUTER):
        rows = jnp.concatenate(line_gather(rows, axes), axis=0)
    return rows


def reduce_all(rows):
    for axes in (OUTER, MIDDLE, INNER):
        rows = line_reduce(jnp.split(rows, SIDE, axis=0), axes)
    return rows


def dense(inputs, targets, w_enc, b_enc, w_self, w_cross, block_ids, w_cross_first):
    first_layer = lax.axis_index("layer") == 0
    width = inputs.shape[2]
    half = width // 2
    blocks = w_enc.shape[2] // BLK
    slots = block_ids.shape[2]
    tail = jnp.pad(block_ids[0].astype(BF16), ((0, 0), (0, BLK - slots)))
    gathered = gather_all(jnp.concatenate([inputs[0], tail], axis=1))
    x, ids = gathered[:, :width], gathered[:, width : width + slots].astype(jnp.int32)
    own_blocks = lax.axis_index("feat") * blocks + jnp.arange(blocks, dtype=jnp.int32)
    hit = ids[:, :, None] == own_blocks[None, None, :]
    active = jnp.repeat(jnp.any(hit, axis=1), BLK, axis=1).astype(F32)
    pre = dot(x, w_enc[0]) + b_enc[0]
    codes = (active * jax.nn.softplus(pre)).astype(BF16)
    turned = to_second_order(codes)
    earlier = to_second(turned)
    source = jnp.where(first_layer, turned, earlier)
    by_block = codes.reshape(-1, 1, blocks, BLK)
    slotted = jnp.sum(jnp.where(hit[..., None], by_block, 0).astype(F32), axis=2).reshape(-1, slots * BLK)
    w_cross_all = jnp.concatenate([w_cross_first, w_cross], axis=1)
    partial = dot(codes, w_self[0]) + dot(earlier, w_cross_all)
    summed = reduce_all(jnp.concatenate([partial, slotted], axis=1).astype(BF16))
    recon = summed[:, :width]
    picked = summed[:, width:].astype(BF16).reshape(-1, slots, BLK)
    err = gather_all((recon - targets[0].astype(F32)).astype(BF16))
    back = to_first_order(to_first(contract_cols(err, w_cross_all)))
    returned = to_first(err[:, :half])
    term = contract_cols(err, w_self[0])
    grad_self = contract_rows(codes, err).astype(BF16)
    cross_err = jnp.where(first_layer, returned, err[:, half:])
    grad_cross = contract_rows(source, cross_err).astype(BF16)
    code_grads = term + jnp.where(first_layer, back, 0.0)
    pre_grads = (code_grads * active * jax.nn.sigmoid(pre)).astype(BF16)
    grad_enc = contract_rows(x, pre_grads).astype(BF16)
    grad_benc = jnp.sum(pre_grads.astype(F32), axis=0)
    return recon, picked, grad_enc, grad_benc[None], grad_self, grad_cross


def per_device(inputs, targets, w_enc, b_enc, w_self, w_cross, block_ids):
    layer = lax.axis_index("layer")
    shard = lax.axis_index("feat")
    width = inputs.shape[2]
    slots = block_ids.shape[2]
    tokens_dev = inputs.shape[1]

    y, z = shard // (SIDE * SIDE), shard % SIDE
    receivers = [
        jnp.where(layer == 0, shard - z + (z - r) % SIDE, shard + SIDE * SIDE * ((y - r) % SIDE - y))
        for r in AWAY
    ]
    scalars = jnp.stack([shard, layer] + receivers).astype(jnp.int32)

    own_ids, other_ids = (ids[0].astype(BF16) + 1 for ids in (block_ids, swapped(block_ids)))
    owner = jnp.full((tokens_dev, 1), shard + 1).astype(BF16)
    place = jnp.arange(tokens_dev, dtype=jnp.int32)[:, None].astype(BF16)
    spare = jnp.zeros((tokens_dev, BLK - 2 * slots - 2), BF16)
    rows = jnp.concatenate([inputs[0], own_ids, other_ids, owner, place, spare], axis=1)

    line = jnp.concatenate(line_gather(rows, INNER), axis=0)
    chosen, pick, spread, flag = select(scalars, line_gather(line, MIDDLE))
    x = ahead(chosen[0], chosen, OUTER)
    x, half_cross = lax.optimization_barrier((x, w_cross))
    w_cross_first = to_second(half_cross)
    codes, gate = encode(scalars, x, w_enc, b_enc, flag, slots)
    other_codes = swapped(codes)
    self_sum, slotted = decode_self(scalars, codes, w_self, slots)
    sums, source, match = decode(scalars, codes, other_codes, self_sum, w_cross_first, w_cross, slotted)
    sums = behind(sums, OUTER)
    exact, sents = line_terms(scalars, behind(spread_sum(scalars, spread, sums, width), MIDDLE), targets)
    err_line, own_err, tail = settle(scalars, exact, ahead(exact, sents, INNER)[1:], tokens_dev, width)
    err_plane = line_gather(err_line, MIDDLE)
    kept = compact(scalars, pick, err_plane)
    errs = ahead(kept[0], kept, OUTER)
    returned = to_first(cross_back(scalars, match, errs, w_cross_first, w_cross))
    term, grad_self = self_back(scalars, codes, errs, w_self)
    grad_enc, grad_benc, grad_cross, picked, recon, again = last(
        scalars, term, gate, source, returned, tail, own_err, targets, x, errs
    )

    def on_every_row(_):
        results = dense(inputs, targets, w_enc, b_enc, w_self, w_cross, block_ids, w_cross_first)
        recon, picked, grad_enc, grad_benc, grad_self, grad_cross = results
        return jnp.int32(0), recon[None], picked.reshape(-1, BLK), grad_enc[None], grad_benc, grad_self[None], grad_cross

    results = (again[0], recon, picked, grad_enc, grad_benc, grad_self, grad_cross)
    _, recon, picked, *grads = lax.while_loop(lambda carried: carried[0] > 0, on_every_row, results)
    return recon, picked.reshape(1, tokens_dev, slots, BLK), *grads


def solution(mesh):
    placed = (
        P("layer", "feat", None),
        P("layer", "feat", None),
        P("layer", None, "feat"),
        P("layer", "feat"),
        P("layer", "feat", None),
        P("feat", "layer"),
        P("layer", "feat", None),
    )
    return jax.shard_map(
        per_device,
        mesh=mesh,
        in_specs=placed,
        out_specs=(
            P("layer", "feat", None),
            P("layer", "feat", None, None),
            P("layer", None, "feat"),
            P("layer", "feat"),
            P("layer", "feat", None),
            P("feat", "layer"),
        ),
        check_vma=False,
    )
```
